256 devices in a mesh: az: 16 (over x_lo, y, core), rad: 8 (over z), dep: 2 (over x_hi).
Axes of the slice: x: 4 (x_hi: 2, x_lo: 2; x = x_hi * 2 + x_lo), y: 4, z: 8, core: 2. Of those that a mesh axis runs over, the one named last changes fastest.
Arguments:
- forward_state: float32 [9, 256, 32, 256], P(None, 'az', 'rad', 'dep'), may hold values from -6 to 6
- forward_memory: float32 [3, 6, 256, 32, 256], P(None, None, 'az', 'rad', 'dep'), may hold values from -3 to 3
- adjoint_state: float32 [9, 256, 32, 256], P(None, 'az', 'rad', 'dep'), may hold values from -6 to 6
- adjoint_memory: float32 [3, 6, 256, 32, 256], P(None, None, 'az', 'rad', 'dep'), may hold values from -3 to 3
- shear_modulus: float32 [256, 32, 256], P('az', 'rad', 'dep'), may hold values from 0.5 to 2
- zone: int32 [256, 32, 256], P('az', 'rad', 'dep'), may hold values from 0 to 7
- zone_elastic: float32 [2, 8], replicated, may hold values from 0.5 to 2
- zone_rates: float32 [3, 8], replicated, may hold values from 0.25 to 4
- zone_weights: float32 [3, 8], replicated, may hold values from 0.1 to 1
- source_cells: int32 [16], replicated, may hold values from 0 to 2097151
- source_force: float32 [2, 3, 16], replicated, may hold values from -16 to 16
- receiver_cells: int32 [256], replicated, may hold values from 0 to 2097151
- receiver_residual: float32 [2, 3, 256], replicated, may hold values from -16 to 16
Outputs:
- gradient: float32 [256, 32, 256], P('az', 'rad', 'dep')
- adjoint_out: float32 [9, 256, 32, 256], P(None, 'az', 'rad', 'dep')
The draws below stay inside these ranges and needn't reach their ends.
Inputs may be any that keep to these rules, and one draw needn't show every extreme that they name: `source_cells`: flat cell index (a * 32 + r) * 256 + z; cells may repeat. `receiver_cells`: flat cell index (a * 32 + r) * 256 + z; cells may repeat.
All inputs are finite; a program needn't handle non-finite values.
Results may differ from the reference program's by a relative error of at most 0.0003.
Values sent between devices are 32-bit elements; how exact they have to be, the bound alone decides.
A program may use at most 128 MiB of HBM per device.

```python
import math
import jax
import jax.numpy as jnp
from jax import lax

STEPS = 2
ZONES = 8
NSRC = 16
NREC = 256
NA = 256
NR = 32
NZ = 256


def place_ends(drawn, stream_key, smallest, high):
    dims = drawn.shape
    spot = [jax.random.randint(jax.random.fold_in(stream_key, axis), (), 0, dims[axis]) for axis in range(len(dims))]
    drawn = drawn.at[tuple(spot)].set(smallest)
    longest = dims.index(max(dims))
    spot[longest] = (spot[longest] + 1) % dims[longest]
    return drawn.at[tuple(spot)].set(high)


def steps_of(own_key, extent, split, least, high):
    loudness = 1.0
    for axis_at, shards_of in split:
        draws = jax.random.uniform(jax.random.fold_in(jax.random.fold_in(own_key, 6), axis_at), (shards_of,), jnp.float32, least / len(split), high / len(split))
        loudness = loudness * jnp.repeat(jnp.exp(draws), extent[axis_at] // shards_of).reshape((-1,) + (1,) * (len(extent) - 1 - axis_at))
    return loudness


def normal_values(own_key, dims, deviation, bound, cuts=(), kind=jnp.bfloat16):
    loudness = steps_of(own_key, dims, cuts, -0.22, 0.18) if cuts else 1.0
    entries = jax.random.normal(own_key, dims, jnp.float32) * deviation * loudness
    return jnp.minimum(jnp.maximum(entries, -bound), bound).astype(kind)


def setup_inputs(seed: int = 0) -> dict:
    keys = jax.random.split(jax.random.key(seed), 14)
    return {
        "forward_state": normal_values(keys[0], (9, NA, NR, NZ), 1.0, 6.0, ((1, 16), (2, 8), (3, 2)), jnp.float32),
        "forward_memory": normal_values(keys[1], (3, 6, NA, NR, NZ), 0.5, 3.0, ((2, 16), (3, 8), (4, 2)), jnp.float32),
        "adjoint_state": normal_values(keys[2], (9, NA, NR, NZ), 1.0, 6.0, ((1, 16), (2, 8), (3, 2)), jnp.float32),
        "adjoint_memory": normal_values(keys[3], (3, 6, NA, NR, NZ), 0.5, 3.0, ((2, 16), (3, 8), (4, 2)), jnp.float32),
        "shear_modulus": jnp.clip(0.5 + 1.5 * jax.random.uniform(keys[4], (NA, NR, NZ), jnp.float32) ** steps_of(keys[4], (NA, NR, NZ), ((0, 16), (1, 8), (2, 2)), -0.2, 0.2), 0.5, 2.0),
        "zone": place_ends(jax.random.randint(keys[5], (NA, NR, NZ), 0, ZONES), jax.random.fold_in(keys[5], 1), 0, ZONES - 1).astype(jnp.int32),
        "zone_elastic": jnp.clip(jax.random.uniform(keys[6], (2, ZONES), jnp.float32, 0.5, 2.0), 0.5, 2.0),
        "zone_rates": jnp.clip(jnp.exp(jax.random.uniform(keys[7], (3, ZONES), jnp.float32, math.log(0.25), math.log(4.0))), 0.25, 4.0),
        "zone_weights": jnp.clip(jax.random.uniform(keys[8], (3, ZONES), jnp.float32, 0.1, 1.0), 0.1, 1.0),
        "source_cells": place_ends(jax.random.randint(keys[9], (NSRC,), 0, NA * NR * NZ), jax.random.fold_in(keys[9], 1), 0, (NA * NR * NZ) - 1).astype(jnp.int32),
        "source_force": normal_values(keys[10], (STEPS, 3, NSRC), 4.0, 16.0, (), jnp.float32),
        "receiver_cells": place_ends(jax.random.randint(keys[11], (NREC,), 0, NA * NR * NZ), jax.random.fold_in(keys[11], 1), 0, (NA * NR * NZ) - 1).astype(jnp.int32),
        "receiver_residual": normal_values(keys[12], (STEPS, 3, NREC), 4.0, 16.0, (), jnp.float32),
    }


time_step = 0.2
coef_near = 1.125
coef_far = 1.0 / 24.0


def offsets(padded, along):
    length = padded.shape[along] - 4
    return [lax.slice_in_dim(padded, offset, offset + length, axis=along) for offset in range(5)]


def trimmed(result, along):
    for across in range(3):
        if across != along:
            result = lax.slice_in_dim(result, 2, result.shape[across] - 2, axis=across)
    return result


def forward_diff(padded, along):
    shifted = offsets(padded, along)
    return trimmed(coef_near * (shifted[3] - shifted[2]) - coef_far * (shifted[4] - shifted[1]), along)


def backward_diff(padded, along):
    shifted = offsets(padded, along)
    return trimmed(coef_near * (shifted[2] - shifted[1]) - coef_far * (shifted[3] - shifted[0]), along)


def middle(padded):
    return padded[2:-2, 2:-2, 2:-2]


def accelerate(velocity, stress_pad, buoyancy, centre, staggered, cell_angle):
    pieces = [stress_pad[comp_index] for comp_index in range(6)]
    push_radial = forward_diff(pieces[0], 1) + backward_diff(pieces[3], 0) / (staggered * cell_angle) + backward_diff(pieces[4], 2) + (middle(pieces[0]) - middle(pieces[1])) / staggered
    push_around = backward_diff(pieces[3], 1) + forward_diff(pieces[1], 0) / (centre * cell_angle) + backward_diff(pieces[5], 2) + 2.0 * middle(pieces[3]) / centre
    push_vertical = backward_diff(pieces[4], 1) + backward_diff(pieces[5], 0) / (centre * cell_angle) + forward_diff(pieces[2], 2) + middle(pieces[4]) / centre
    return velocity + time_step * buoyancy * jnp.stack([push_radial, push_around, push_vertical])


def strain_rates(velocity_pad, centre, staggered, cell_angle):
    v_radial, v_around, v_vertical = velocity_pad[0], velocity_pad[1], velocity_pad[2]
    rate_rr = backward_diff(v_radial, 1)
    rate_tt = backward_diff(v_around, 0) / (centre * cell_angle) + middle(v_radial) / centre
    rate_zz = backward_diff(v_vertical, 2)
    rate_rt = 0.5 * (forward_diff(v_around, 1) + forward_diff(v_radial, 0) / (staggered * cell_angle) - middle(v_around) / staggered)
    rate_rz = 0.5 * (forward_diff(v_radial, 2) + forward_diff(v_vertical, 1))
    rate_tz = 0.5 * (forward_diff(v_around, 2) + forward_diff(v_vertical, 0) / (centre * cell_angle))
    return jnp.stack([rate_rr, rate_tt, rate_zz, rate_rt, rate_rz, rate_tz])


def relax_stress(stress, memory, strain, lame_first, shear, relax_rates, weights):
    dilation = strain[0] + strain[1] + strain[2]
    doubled = 2.0 * shear
    elastic = jnp.stack([lame_first * dilation + doubled * strain[0], lame_first * dilation + doubled * strain[1], lame_first * dilation + doubled * strain[2], doubled * strain[3], doubled * strain[4], doubled * strain[5]])
    memory = memory + time_step * relax_rates[:, None] * (weights[:, None] * elastic[None] - memory)
    stress = stress + time_step * (elastic - (memory[0] + memory[1] + memory[2]))
    return stress, memory


def materials(zone, zone_elastic, zone_rates, zone_weights):
    zone_table = jnp.concatenate([zone_elastic, zone_rates, zone_weights], axis=0)
    looked_up = jnp.zeros((zone_table.shape[0],) + zone.shape, zone_table.dtype)
    for zone_number in range(zone_table.shape[1]):
        looked_up = jnp.where((zone == zone_number)[None], zone_table[:, zone_number].reshape(-1, 1, 1, 1), looked_up)
    return looked_up[0], looked_up[1], looked_up[2:5], looked_up[5:8]


def kernel_term(forward_strain, adjoint_strain):
    fwd_rates, adj_rates = forward_strain, adjoint_strain
    return time_step * 2.0 * (fwd_rates[0] * adj_rates[0] + fwd_rates[1] * adj_rates[1] + fwd_rates[2] * adj_rates[2] + 2.0 * (fwd_rates[3] * adj_rates[3] + fwd_rates[4] * adj_rates[4] + fwd_rates[5] * adj_rates[5]))


def pad_full(field):
    field = jnp.pad(field, ((0, 0), (2, 2), (0, 0), (0, 0)), mode="wrap")
    return jnp.pad(field, ((0, 0), (0, 0), (2, 2), (2, 2)))


def inject_all(velocity, cell_list, forcing, buoyancy):
    flattened = velocity.reshape(3, -1)
    picked = buoyancy.reshape(-1)[cell_list]
    flattened = flattened.at[:, cell_list].add(time_step * picked[None, :] * forcing)
    return flattened.reshape(velocity.shape)


def reference(forward_state, forward_memory, adjoint_state, adjoint_memory, shear_modulus, zone, zone_elastic, zone_rates, zone_weights, source_cells, source_force, receiver_cells, receiver_residual):
    lame_first, buoyancy, relax_rates, weights = materials(zone, zone_elastic, zone_rates, zone_weights)
    cell_angle = 2.0 * math.pi / NA
    inner_radius = NA / (2.0 * math.pi)
    centre = inner_radius + jnp.arange(NR).astype(jnp.float32).reshape(1, -1, 1)
    staggered = centre + 0.5
    systems = [[forward_state, forward_memory, source_cells, source_force, [], False], [adjoint_state, adjoint_memory, receiver_cells, receiver_residual, [], True]]
    for system in systems:
        for moment in range(STEPS):
            current = system[0]
            velocity = accelerate(current[:3], pad_full(current[3:]), buoyancy, centre, staggered, cell_angle)
            velocity = inject_all(velocity, system[2], system[3][moment], buoyancy)
            strain = strain_rates(pad_full(velocity), centre, staggered, cell_angle)
            system[4].append(strain)
            if moment + 1 < STEPS or system[5]:
                stress, memory = relax_stress(current[3:], system[1], strain, lame_first, shear_modulus, relax_rates, weights)
                system[0] = jnp.concatenate([velocity, stress], axis=0)
                system[1] = memory
            else:
                system[0] = velocity
    gradient = kernel_term(systems[0][4][STEPS - 1], systems[1][4][0])
    for moment in range(1, STEPS):
        gradient = gradient + kernel_term(systems[0][4][STEPS - 1 - moment], systems[1][4][moment])
    return gradient, systems[1][0]
```

```python
import math

import jax
import jax.numpy as jnp
from jax import lax
from jax.experimental import pallas as pl
from jax.experimental.pallas import tpu as pltpu
from jax.sharding import PartitionSpec as P

MESH = pl.DeviceIdType.MESH
f32 = jnp.float32

DT = 0.2
C1 = 1.125
C2 = 1.0 / 24.0

RR, RZ, RT, TT, TZ, ZZ = range(6)
IN_STATE = {RR: 3, TT: 4, ZZ: 5, RT: 6, RZ: 7, TZ: 8}
STRAIN_ORDER = (RR, TT, ZZ, RT, RZ, TZ)

ADJ, FWD = 0, 1
NAZ, NRAD, LANES = 16, 4, 128
LO, HI = 8, 8 + NAZ
R0 = 2


def forward4(before, here, after, after2):
    return C1 * (after - here) - C2 * (after2 - before)


def backward4(before2, before, here, after):
    return C1 * (here - before) - C2 * (after - before2)


def kernel(
    fs, fm, as_, am, mu_h, zone_h, ze_h, zr_h, zw_h, sc_h, sf_h, rc_h, rr_h,
    grad_h, adj_h,
    raw, mem, mu_v, zone_v, ze, zr, zw, sc_v, sf_v, rc_v, rr_v,
    stress, vel, dz, msg_out, msg_in, strain, a1, a2, inj, geo, mat, out_v, grad_v,
    in_sem, out_sem, send_sem, recv_sem,
):
    n_az, n_rad, n_dep = lax.axis_size("az"), lax.axis_size("rad"), lax.axis_size("dep")
    az, rad, dep = lax.axis_index("az"), lax.axis_index("rad"), lax.axis_index("dep")
    az_up, az_dn = {"az": lax.rem(az + 1, n_az)}, {"az": lax.rem(az + n_az - 1, n_az)}
    rad_up, rad_dn = {"rad": lax.rem(rad + 1, n_rad)}, {"rad": lax.rem(rad + n_rad - 1, n_rad)}
    dep_other = {"dep": 1 - dep}

    pending = []

    def bring(src, dst):
        copy = pltpu.make_async_copy(src, dst, in_sem.at[len(pending)])
        copy.start()
        pending.append(copy)
        return copy

    states = (as_, fs)
    memories = (am, fm)
    got_stress = [bring(states[s].at[pl.ds(3, 6)], raw.at[s, pl.ds(3, 6)]) for s in (ADJ, FWD)]

    barrier = pltpu.get_barrier_semaphore()
    for place in (az_up, az_dn, rad_up, rad_dn, dep_other):
        pl.semaphore_signal(barrier, inc=1, device_id=place, device_id_type=MESH)

    got_small = [
        bring(a, b)
        for a, b in (
            (ze_h, ze), (zr_h, zr), (zw_h, zw), (sc_h, sc_v), (sf_h, sf_v), (rc_h, rc_v),
            (rr_h, rr_v), (zone_h, zone_v), (mu_h, mu_v),
        )
    ]
    got_vel = [bring(states[s].at[pl.ds(0, 3)], raw.at[s, pl.ds(0, 3)]) for s in (ADJ, FWD)]
    got_mem = [bring(memories[s], mem.at[s]) for s in (ADJ, FWD)]

    lane = lax.broadcasted_iota(jnp.int32, (NAZ, LANES), 1)
    lane8 = lax.broadcasted_iota(jnp.int32, (8, LANES), 1)

    def where_f(cond, value):
        return jnp.where(cond, f32(value), f32(0.0))

    def pack_depth(sys, phase, fields):
        parcel = None
        for t, (get, ahead) in enumerate(fields):
            for r in range(NRAD):
                g = get(r)
                m1 = pltpu.roll(g, LANES - 1, 1)
                r1 = pltpu.roll(g, 1, 1)
                if ahead:
                    m2 = pltpu.roll(g, LANES - 2, 1)
                    stay = (where_f(lane < 127, C1) * m1 - C1 * g - where_f(lane < 126, C2) * m2
                            + where_f(lane >= 1, C2) * r1)
                    wrap = (where_f(lane == 127, C1) * m1 - where_f(lane >= 126, C2) * m2
                            + where_f(lane == 0, C2) * r1)
                else:
                    r2 = pltpu.roll(g, 2, 1)
                    stay = (C1 * g - where_f(lane >= 1, C1) * r1 - where_f(lane < 127, C2) * m1
                            + where_f(lane >= 2, C2) * r2)
                    wrap = (where_f(lane <= 1, C2) * r2 - where_f(lane == 0, C1) * r1
                            - where_f(lane == 127, C2) * m1)
                dz[sys, t, r] = stay
                for half in range(2):
                    shift = 12 * (2 * r + half) + 4 * t
                    piece = wrap[8 * half: 8 * half + 8]
                    if shift:
                        piece = pltpu.roll(piece, shift, 1)
                    parcel = piece if parcel is None else parcel + piece
        msg_out[sys, phase] = parcel

    mine = lane8 - 126 * (1 - dep)
    edge = (mine >= 0) & (mine < 2)

    def depth_diff(sys, parcel, t, r):
        halves = []
        for half in range(2):
            shift = 12 * (2 * r + half) + 4 * t
            piece = pltpu.roll(parcel, (LANES - shift) % LANES, 1) if shift else parcel
            halves.append(jnp.where(edge, piece, 0.0))
        return dz[sys, t, r] + jnp.concatenate(halves, axis=0)

    own = pl.ds(LO, NAZ)
    own_r = pl.ds(R0, NRAD)
    started = []

    def exchange(sys, phase, field, rad_plan, az_from, az_count):
        legs = []

        def leg(src, dst, place):
            number = len(legs)
            copy = pltpu.make_async_remote_copy(
                src_ref=src, dst_ref=dst, send_sem=send_sem.at[sys, phase, number],
                recv_sem=recv_sem.at[sys, phase, number], device_id=place, device_id_type=MESH,
            )
            copy.start()
            legs.append(copy)
            started.append(copy)

        comps = pl.ds(az_from, az_count)
        leg(field.at[comps, own_r, pl.ds(HI - 8, 8)], field.at[comps, own_r, pl.ds(0, 8)], az_up)
        leg(field.at[comps, own_r, pl.ds(LO, 8)], field.at[comps, own_r, pl.ds(HI, 8)], az_dn)
        for first, count, up, down in rad_plan:
            comps_r = pl.ds(first, count)
            leg(field.at[comps_r, pl.ds(R0 + NRAD - up, up), own],
                field.at[comps_r, pl.ds(R0 - up, up), own], rad_up)
            leg(field.at[comps_r, pl.ds(R0, down), own],
                field.at[comps_r, pl.ds(R0 + NRAD, down), own], rad_dn)
        leg(msg_out.at[sys, phase], msg_in.at[sys, phase], dep_other)
        return legs

    def arrive(legs, field, comps):
        for copy in legs:
            copy.wait_recv()

        @pl.when(rad == 0)
        def _():
            field[pl.ds(0, comps), pl.ds(0, R0), own] = jnp.zeros((comps, R0, NAZ, LANES), f32)

        @pl.when(rad == n_rad - 1)
        def _():
            field[pl.ds(0, comps), pl.ds(R0 + NRAD, 2), own] = jnp.zeros((comps, 2, NAZ, LANES), f32)

    def rows(r):
        return pl.ds(r, NAZ, stride=NRAD)

    def stress_field(sys, step):
        return stress.at[sys, step]

    def vel_field(sys, step):
        return vel.at[sys, step]

    def send_stress(sys, step):
        field = stress_field(sys, step)
        pack_depth(sys, 2 * step, [
            (lambda r: field[RZ, R0 + r, LO:HI], False),
            (lambda r: field[TZ, R0 + r, LO:HI], False),
            (lambda r: field[ZZ, R0 + r, LO:HI], True),
        ])
        return exchange(sys, 2 * step, field, ((RR, 1, 1, 2), (RZ, 2, 2, 1)), RT, 3)

    def send_vel(sys, step):
        field = vel_field(sys, step)
        pack_depth(sys, 2 * step + 1, [
            (lambda r: field[2, R0 + r, LO:HI], False),
            (lambda r: field[0, R0 + r, LO:HI], True),
            (lambda r: field[1, R0 + r, LO:HI], True),
        ])
        return exchange(sys, 2 * step + 1, field, ((0, 1, 2, 1), (1, 2, 1, 2)), 0, 3)

    def rad4(field, c, r, first):
        return [field[c, R0 + r + first + i, LO:HI] for i in range(4)]

    def az4(field, c, r, first):
        return [field[c, R0 + r, LO + first + i: HI + first + i] for i in range(4)]

    def velocity_update(sys, step):
        field, new = stress_field(sys, step), vel_field(sys, step)
        parcel = msg_in[sys, 2 * step]
        for r in range(NRAD):
            inv_s, inv_c, inv_sa, inv_ca = [geo[i, r] for i in range(4)]
            if step == 0:
                old = [raw[sys, c, rows(r)] for c in range(3)]
            else:
                old = [vel[sys, 0, c, R0 + r, LO:HI] for c in range(3)]
            s_rr, s_tt = field[RR, R0 + r, LO:HI], field[TT, R0 + r, LO:HI]
            s_rt, s_rz = field[RT, R0 + r, LO:HI], field[RZ, R0 + r, LO:HI]
            push = [
                forward4(*rad4(field, RR, r, -1)) + backward4(*az4(field, RT, r, -2)) * inv_sa
                + depth_diff(sys, parcel, 0, r) + (s_rr - s_tt) * inv_s,
                backward4(*rad4(field, RT, r, -2)) + forward4(*az4(field, TT, r, -1)) * inv_ca
                + depth_diff(sys, parcel, 1, r) + 2.0 * s_rt * inv_c,
                backward4(*rad4(field, RZ, r, -2)) + backward4(*az4(field, TZ, r, -2)) * inv_ca
                + depth_diff(sys, parcel, 2, r) + s_rz * inv_c,
            ]
            gain = mat[0, r]
            for c in range(3):
                new[c, R0 + r, LO:HI] = old[c] + gain * (push[c] + inj[sys, step, c, r])

    def strain_at(sys, step, parcel, r):
        field = vel_field(sys, step)
        inv_s, inv_c, inv_sa, inv_ca = [geo[i, r] for i in range(4)]
        v_r, v_t = field[0, R0 + r, LO:HI], field[1, R0 + r, LO:HI]
        return [
            backward4(*rad4(field, 0, r, -2)),
            backward4(*az4(field, 1, r, -2)) * inv_ca + v_r * inv_c,
            depth_diff(sys, parcel, 0, r),
            0.5 * (forward4(*rad4(field, 1, r, -1)) + forward4(*az4(field, 0, r, -1)) * inv_sa
                   - v_t * inv_s),
            0.5 * (depth_diff(sys, parcel, 1, r) + forward4(*rad4(field, 2, r, -1))),
            0.5 * (depth_diff(sys, parcel, 2, r) + forward4(*az4(field, 2, r, -1)) * inv_ca),
        ]

    def load_state(sys):
        got_stress[sys].wait()
        field = stress_field(sys, 0)
        for c in range(6):
            for r in range(NRAD):
                field[c, R0 + r, LO:HI] = raw[sys, IN_STATE[c], rows(r)]

    load_state(ADJ)
    pl.semaphore_wait(barrier, 5)
    legs_s = [None, None]
    legs_v = [None, None]
    legs_s[ADJ] = send_stress(ADJ, 0)
    load_state(FWD)
    legs_s[FWD] = send_stress(FWD, 0)

    for copy in got_small:
        copy.wait()
    angle = 2.0 * math.pi / (NAZ * n_az)
    inner = (NAZ * n_az) / (2.0 * math.pi)
    for r in range(NRAD):
        centre = jnp.full((NAZ, LANES), f32(inner), f32) + (rad * NRAD + r).astype(f32)
        staggered = centre + 0.5
        geo[0, r] = 1.0 / staggered
        geo[1, r] = 1.0 / centre
        geo[2, r] = 1.0 / (staggered * angle)
        geo[3, r] = 1.0 / (centre * angle)

    betas = []
    for r in range(NRAD):
        zone = zone_v[rows(r)]
        looked = [jnp.zeros((NAZ, LANES), f32) for _ in range(8)]
        for number in range(8):
            hit = zone == number
            for t in range(8):
                ref, row = (ze, t) if t < 2 else (zr, t - 2) if t < 5 else (zw, t - 5)
                looked[t] = jnp.where(hit, ref[row, number], looked[t])
        lame, buoyancy = looked[0], looked[1]
        alpha = [DT * looked[2 + i] for i in range(3)]
        weight = looked[5:8]
        beta = [1.0 - a for a in alpha]
        share = [a * w for a, w in zip(alpha, weight)]
        gain = DT * (1.0 - (share[0] + share[1] + share[2]))
        later = DT * (beta[0] * share[0] + beta[1] * share[1] + beta[2] * share[2])
        doubled = 2.0 * mu_v[rows(r)]
        mat[0, r] = DT * buoyancy
        mat[1, r] = gain * lame
        mat[2, r] = gain * doubled
        mat[3, r] = later * lame
        mat[4, r] = later * doubled
        for i in range(3):
            mat[5 + i, r] = beta[i]

    def inject(sys, cells_ref, force_ref, count):
        cells = cells_ref[...]
        around = lax.shift_right_logical(cells, 13) - NAZ * az
        radial = (lax.shift_right_logical(cells, 8) & 31) - NRAD * rad
        depth = (cells & 255) - LANES * dep
        inside = (around >= 0) & (around < NAZ) & (radial >= 0) & (radial < NRAD)
        key = jnp.where(inside, radial * NAZ + around, -1)
        here = lax.broadcasted_iota(jnp.int32, (NRAD * NAZ, count), 0) == key
        lanes = (lax.broadcasted_iota(jnp.int32, (LANES, count), 0) == depth).astype(f32)
        for step in range(2):
            for c in range(3):
                picked = jnp.where(here, force_ref[c, step: step + 1, :], 0.0)
                total = lax.dot_general(
                    picked, lanes, (((1,), (1,)), ((), ())),
                    precision=lax.Precision.HIGHEST, preferred_element_type=f32,
                )
                for r in range(NRAD):
                    inj[sys, step, c, r] = total[r * NAZ: (r + 1) * NAZ]

    inject(ADJ, rc_v, rr_v, rc_v.shape[1])
    inject(FWD, sc_v, sf_v, sc_v.shape[1])
    for sys in (ADJ, FWD):
        got_vel[sys].wait()

    def advance_velocity(sys, step):
        arrive(legs_s[sys], stress_field(sys, step), 3)
        velocity_update(sys, step)
        legs_v[sys] = send_vel(sys, step)

    for sys in (ADJ, FWD):
        advance_velocity(sys, 0)

    for sys in (ADJ, FWD):
        got_mem[sys].wait()
        for r in range(NRAD):
            beta = [mat[5 + i, r] for i in range(3)]
            for e in range(6):
                m = [beta[i] * mem[sys, 6 * i + e, rows(r)] for i in range(3)]
                a1[sys, e, r] = raw[sys, 3 + e, rows(r)] - DT * (m[0] + m[1] + m[2])
                if sys == ADJ:
                    a2[e, r] = DT * (beta[0] * m[0] + beta[1] * m[1] + beta[2] * m[2])

    def first_stress(sys):
        arrive(legs_v[sys], vel_field(sys, 0), 3)
        parcel = msg_in[sys, 1]
        new = stress_field(sys, 1)
        for r in range(NRAD):
            e = strain_at(sys, 0, parcel, r)
            dilation = e[0] + e[1] + e[2]
            common = mat[1, r] * dilation
            gm = mat[2, r]
            for i in range(6):
                strain[sys, 0, i, r] = e[i]
                change = gm * e[i] + common if i < 3 else gm * e[i]
                new[STRAIN_ORDER[i], R0 + r, LO:HI] = a1[sys, i, r] + change
        legs_s[sys] = send_stress(sys, 1)

    for sys in (ADJ, FWD):
        first_stress(sys)

    for r in range(NRAD):
        e = [strain[ADJ, 0, i, r] for i in range(6)]
        common = mat[3, r] * (e[0] + e[1] + e[2])
        hm = mat[4, r]
        for i in range(6):
            drop = hm * e[i] + common if i < 3 else hm * e[i]
            a2[i, r] = stress[ADJ, 1, STRAIN_ORDER[i], R0 + r, LO:HI] - a2[i, r] - drop

    for sys in (ADJ, FWD):
        advance_velocity(sys, 1)
    for r in range(NRAD):
        for c in range(3):
            out_v[c, rows(r)] = vel[ADJ, 1, c, R0 + r, LO:HI]
    out_vel = pltpu.make_async_copy(out_v.at[pl.ds(0, 3)], adj_h.at[pl.ds(0, 3)], out_sem.at[0])
    out_vel.start()

    def product(e, f):
        return 2.0 * DT * (e[0] * f[0] + e[1] * f[1] + e[2] * f[2]
                           + 2.0 * (e[3] * f[3] + e[4] * f[4] + e[5] * f[5]))

    arrive(legs_v[ADJ], vel_field(ADJ, 1), 3)
    parcel = msg_in[ADJ, 3]
    for r in range(NRAD):
        e = strain_at(ADJ, 1, parcel, r)
        common = mat[1, r] * (e[0] + e[1] + e[2])
        gm = mat[2, r]
        for i in range(6):
            change = gm * e[i] + common if i < 3 else gm * e[i]
            out_v[3 + i, rows(r)] = a2[i, r] + change
        a1[ADJ, 0, r] = product(e, [strain[FWD, 0, i, r] for i in range(6)])
    out_stress = pltpu.make_async_copy(out_v.at[pl.ds(3, 6)], adj_h.at[pl.ds(3, 6)], out_sem.at[1])
    out_stress.start()

    arrive(legs_v[FWD], vel_field(FWD, 1), 3)
    parcel = msg_in[FWD, 3]
    for r in range(NRAD):
        e = strain_at(FWD, 1, parcel, r)
        grad_v[rows(r)] = a1[ADJ, 0, r] + product(e, [strain[ADJ, 0, i, r] for i in range(6)])
    out_grad = pltpu.make_async_copy(grad_v, grad_h, out_sem.at[2])
    out_grad.start()

    for copy in started:
        copy.wait_send()
    out_vel.wait()
    out_stress.wait()
    out_grad.wait()


def shards(
    forward_state, forward_memory, adjoint_state, adjoint_memory, shear_modulus, zone,
    zone_elastic, zone_rates, zone_weights, source_cells, source_force, receiver_cells,
    receiver_residual,
):
    cells = NAZ * NRAD
    nsrc, nrec = source_cells.shape[0], receiver_cells.shape[0]
    block = (NRAD, NAZ, LANES)
    vmem = pltpu.VMEM
    hbm = pl.BlockSpec(memory_space=pltpu.HBM)
    gradient, adjoint_out = pl.pallas_call(
        kernel,
        out_shape=(
            jax.ShapeDtypeStruct((cells, LANES), f32),
            jax.ShapeDtypeStruct((9, cells, LANES), f32),
        ),
        in_specs=[hbm] * 13,
        out_specs=(hbm, hbm),
        scratch_shapes=[
            vmem((2, 9, cells, LANES), f32),
            vmem((2, 18, cells, LANES), f32),
            vmem((cells, LANES), f32),
            vmem((cells, LANES), jnp.int32),
            pltpu.SMEM((2, 8), f32),
            pltpu.SMEM((3, 8), f32),
            pltpu.SMEM((3, 8), f32),
            vmem((1, nsrc), jnp.int32),
            vmem((3, 2, nsrc), f32),
            vmem((1, nrec), jnp.int32),
            vmem((3, 2, nrec), f32),
            vmem((2, 2, 6, NRAD + 4, NAZ + 16, LANES), f32),
            vmem((2, 2, 3, NRAD + 4, NAZ + 16, LANES), f32),
            vmem((2, 3) + block, f32),
            vmem((2, 4, 8, LANES), f32),
            vmem((2, 4, 8, LANES), f32),
            vmem((2, 1, 6) + block, f32),
            vmem((2, 6) + block, f32),
            vmem((6,) + block, f32),
            vmem((2, 2, 3) + block, f32),
            vmem((4,) + block, f32),
            vmem((8,) + block, f32),
            vmem((9, cells, LANES), f32),
            vmem((cells, LANES), f32),
            pltpu.SemaphoreType.DMA((16,)),
            pltpu.SemaphoreType.DMA((3,)),
            pltpu.SemaphoreType.DMA((2, 4, 7)),
            pltpu.SemaphoreType.DMA((2, 4, 7)),
        ],
        compiler_params=pltpu.CompilerParams(
            collective_id=0, has_side_effects=True, vmem_limit_bytes=60 * 2**20
        ),
        name="window",
    )(
        forward_state.reshape(9, cells, LANES),
        forward_memory.reshape(18, cells, LANES),
        adjoint_state.reshape(9, cells, LANES),
        adjoint_memory.reshape(18, cells, LANES),
        shear_modulus.reshape(cells, LANES),
        zone.reshape(cells, LANES),
        zone_elastic, zone_rates, zone_weights,
        source_cells.reshape(1, nsrc), source_force.transpose(1, 0, 2),
        receiver_cells.reshape(1, nrec), receiver_residual.transpose(1, 0, 2),
    )
    return gradient.reshape(NAZ, NRAD, LANES), adjoint_out.reshape(9, NAZ, NRAD, LANES)


def solution(mesh):
    return jax.shard_map(
        shards,
        mesh=mesh,
        in_specs=(
            P(None, "az", "rad", "dep"),
            P(None, None, "az", "rad", "dep"),
            P(None, "az", "rad", "dep"),
            P(None, None, "az", "rad", "dep"),
            P("az", "rad", "dep"),
            P("az", "rad", "dep"),
            P(), P(), P(), P(), P(), P(), P(),
        ),
        out_specs=(P("az", "rad", "dep"), P(None, "az", "rad", "dep")),
        check_vma=False,
    )
```

```python
import math

import jax
import jax.numpy as jnp
from jax import lax
from jax.experimental import pallas as pl
from jax.experimental.pallas import tpu as pltpu
from jax.sharding import PartitionSpec as P

MESH = pl.DeviceIdType.MESH
f32 = jnp.float32

DT = 0.2
C1 = 1.125
C2 = 1.0 / 24.0

RR, RZ, RT, TT, TZ, ZZ = range(6)
IN_STATE = {RR: 3, TT: 4, ZZ: 5, RT: 6, RZ: 7, TZ: 8}
STRAIN_ORDER = (RR, TT, ZZ, RT, RZ, TZ)

ADJ, FWD = 0, 1
NAZ, NRAD, LANES = 16, 4, 128
LO, HI = 8, 8 + NAZ
R0 = 2


class View:
    def __init__(self, ref, sys, step):
        self.ref, self.lead = ref, (sys, step)

    def __getitem__(self, index):
        return self.ref[self.lead + index]

    def __setitem__(self, index, value):
        self.ref[self.lead + index] = value

    def slab(self, index):
        return self.ref.at[self.lead + index]


def forward4(before, here, after, after2):
    return C1 * (after - here) - C2 * (after2 - before)


def backward4(before2, before, here, after):
    return C1 * (here - before) - C2 * (after - before2)


def kernel(
    fs, fm, as_, am, mu_h, zone_h, ze_h, zr_h, zw_h, sc_h, sf_h, rc_h, rr_h,
    grad_h, adj_h,
    raw, mem, mu_v, zone_v, ze, zr, zw, sc_v, sf_v, rc_v, rr_v,
    stress, vel, dz, msg_out, msg_in, strain, a1, a2, inj, geo, mat, out_v, grad_v,
    in_sem, out_sem, send_sem, recv_sem,
):
    n_az, n_rad, n_dep = lax.axis_size("az"), lax.axis_size("rad"), lax.axis_size("dep")
    az, rad, dep = lax.axis_index("az"), lax.axis_index("rad"), lax.axis_index("dep")
    az_up, az_dn = {"az": lax.rem(az + 1, n_az)}, {"az": lax.rem(az + n_az - 1, n_az)}
    rad_up, rad_dn = {"rad": rad + 1}, {"rad": rad - 1}
    dep_other = {"dep": 1 - dep}

    has_dn, has_up = rad > 0, rad < n_rad - 1
    barrier = pltpu.get_barrier_semaphore()
    for place in (az_up, az_dn, dep_other):
        pl.semaphore_signal(barrier, inc=1, device_id=place, device_id_type=MESH)

    @pl.when(has_up)
    def _():
        pl.semaphore_signal(barrier, inc=1, device_id=rad_up, device_id_type=MESH)

    @pl.when(has_dn)
    def _():
        pl.semaphore_signal(barrier, inc=1, device_id=rad_dn, device_id_type=MESH)

    pending = []

    def bring(src, dst):
        copy = pltpu.make_async_copy(src, dst, in_sem.at[len(pending)])
        copy.start()
        pending.append(copy)
        return copy

    states = (as_, fs)
    memories = (am, fm)
    got_stress = [bring(states[s].at[pl.ds(3, 6)], raw.at[s, pl.ds(3, 6)]) for s in (ADJ, FWD)]

    got_small = [
        bring(a, b)
        for a, b in (
            (ze_h, ze), (zr_h, zr), (zw_h, zw), (sc_h, sc_v), (sf_h, sf_v), (rc_h, rc_v),
            (rr_h, rr_v), (zone_h, zone_v), (mu_h, mu_v),
        )
    ]
    got_vel = [bring(states[s].at[pl.ds(0, 3)], raw.at[s, pl.ds(0, 3)]) for s in (ADJ, FWD)]
    got_mem = [bring(memories[s], mem.at[s]) for s in (ADJ, FWD)]

    lane = lax.broadcasted_iota(jnp.int32, (NAZ, LANES), 1)
    lane8 = lax.broadcasted_iota(jnp.int32, (8, LANES), 1)

    def where_f(cond, value):
        return jnp.where(cond, f32(value), f32(0.0))

    def base(t, r, half):
        return 12 * (2 * r + half) + 4 * t

    ends = (lane8 < 2) | (lane8 >= 126)

    def pack_depth(sys, phase, gets):
        parcel = None
        for r in range(NRAD):
            for t, get in enumerate(gets):
                g = get(r)
                for half in range(2):
                    piece = jnp.where(ends, g[8 * half: 8 * half + 8], 0.0)
                    if base(t, r, half):
                        piece = pltpu.roll(piece, base(t, r, half), 1)
                    parcel = piece if parcel is None else parcel + piece
        msg_out[sys, phase] = parcel

    def local_depth(sys, gets, aheads):
        for t in range(3):
            for r in range(NRAD):
                g = gets[t](r)
                m1 = pltpu.roll(g, LANES - 1, 1)
                r1 = pltpu.roll(g, 1, 1)
                if aheads[t]:
                    m2 = pltpu.roll(g, LANES - 2, 1)
                    dz[sys, t, r] = (where_f(lane < 127, C1) * m1 - C1 * g - where_f(lane < 126, C2) * m2
                                     + where_f(lane >= 1, C2) * r1)
                else:
                    r2 = pltpu.roll(g, 2, 1)
                    dz[sys, t, r] = (C1 * g - where_f(lane >= 1, C1) * r1 - where_f(lane < 127, C2) * m1
                                     + where_f(lane >= 2, C2) * r2)

    slot = lax.rem(lax.rem(lane8 + 2, LANES), 12)
    place_in = lax.rem(slot, 4)
    which = lax.div(slot, 4)

    def wraps(sys, phase, aheads):
        x = msg_in[sys, phase]
        ahead = None
        for t in range(3):
            if aheads[t]:
                ahead = (which == t) if ahead is None else ahead | (which == t)
        behind = jnp.logical_not(ahead)
        m1, m2 = pltpu.roll(x, LANES - 1, 1), pltpu.roll(x, LANES - 2, 1)
        r1, r2 = pltpu.roll(x, 1, 1), pltpu.roll(x, 2, 1)
        at126, at127, at0, at1 = [place_in == i for i in range(4)]
        k_m1 = jnp.where(at127, jnp.where(ahead, f32(C1), f32(-C2)), 0.0)
        k_m2 = where_f(ahead & (at126 | at127), -C2)
        k_r1 = jnp.where(at0, jnp.where(ahead, f32(C2), f32(-C1)), 0.0)
        k_r2 = where_f(behind & (at0 | at1), C2)
        return k_m1 * m1 + k_m2 * m2 + k_r1 * r1 + k_r2 * r2

    mine = lane8 - 126 * (1 - dep)
    edge = (mine >= 0) & (mine < 2)

    def depth_diff(sys, parcel, t, r):
        halves = []
        for half in range(2):
            shift = base(t, r, half)
            piece = pltpu.roll(parcel, LANES - shift, 1) if shift else parcel
            halves.append(jnp.where(edge, piece, 0.0))
        return dz[sys, t, r] + jnp.concatenate(halves, axis=0)

    own = pl.ds(LO, NAZ)
    own_r = pl.ds(R0, NRAD)
    started = []

    def exchange(sys, phase, field, rad_plan, az_from, az_count):
        number = [0]
        legs, up_legs, dn_legs = [], [], []

        def leg(where, src, dst, place, group):
            n = number[0]
            number[0] += 1

            def make():
                return pltpu.make_async_remote_copy(
                    src_ref=where.slab(src), dst_ref=where.slab(dst),
                    send_sem=send_sem.at[sys, phase, n], recv_sem=recv_sem.at[sys, phase, n],
                    device_id=place, device_id_type=MESH,
                )

            make().start()
            group.append(make)

        @pl.when(has_up)
        def _():
            for first, count, up, down in rad_plan:
                comps = pl.ds(first, count)
                leg(field, (comps, pl.ds(R0 + NRAD - up, up), own), (comps, pl.ds(R0 - up, up), own),
                    rad_up, up_legs)

        @pl.when(has_dn)
        def _():
            for first, count, up, down in rad_plan:
                comps = pl.ds(first, count)
                leg(field, (comps, pl.ds(R0, down), own), (comps, pl.ds(R0 + NRAD, down), own),
                    rad_dn, dn_legs)

        comps = pl.ds(az_from, az_count)
        leg(field, (comps, own_r, pl.ds(HI - 8, 8)), (comps, own_r, pl.ds(0, 8)), az_up, legs)
        leg(field, (comps, own_r, pl.ds(LO, 8)), (comps, own_r, pl.ds(HI, 8)), az_dn, legs)
        legs_msg = number[0]

        def make_depth():
            return pltpu.make_async_remote_copy(
                src_ref=msg_out.at[sys, phase], dst_ref=msg_in.at[sys, phase],
                send_sem=send_sem.at[sys, phase, legs_msg], recv_sem=recv_sem.at[sys, phase, legs_msg],
                device_id=dep_other, device_id_type=MESH,
            )

        make_depth().start()
        legs.append(make_depth)
        groups = legs, up_legs, dn_legs
        started.append(groups)
        return groups

    def arrive(groups):
        legs, up_legs, dn_legs = groups
        for make in legs:
            make().wait_recv()

        @pl.when(has_dn)
        def _():
            for make in up_legs:
                make().wait_recv()

        @pl.when(has_up)
        def _():
            for make in dn_legs:
                make().wait_recv()

    def rows(r):
        return pl.ds(r, NAZ, stride=NRAD)

    def stress_field(sys, step):
        return View(stress, sys, step)

    def vel_field(sys, step):
        return View(vel, sys, step)

    STRESS_AHEAD = (False, False, True)
    VEL_AHEAD = (False, True, True)

    def send_stress(sys, step):
        field = stress_field(sys, step)
        gets = [lambda r, c=c: field[c, R0 + r, LO:HI] for c in (RZ, TZ, ZZ)]
        pack_depth(sys, 2 * step, gets)
        groups = exchange(sys, 2 * step, field, ((RR, 1, 1, 2), (RZ, 2, 2, 1)), RT, 3)
        local_depth(sys, gets, STRESS_AHEAD)
        return groups

    def send_vel(sys, step):
        field = vel_field(sys, step)
        gets = [lambda r, c=c: field[c, R0 + r, LO:HI] for c in (2, 0, 1)]
        pack_depth(sys, 2 * step + 1, gets)
        groups = exchange(sys, 2 * step + 1, field, ((0, 1, 2, 1), (1, 2, 1, 2)), 0, 3)
        local_depth(sys, gets, VEL_AHEAD)
        return groups

    def rad4(field, c, r, first):
        return [field[c, R0 + r + first + i, LO:HI] for i in range(4)]

    def az4(field, c, r, first):
        return [field[c, R0 + r, LO + first + i: HI + first + i] for i in range(4)]

    def velocity_update(sys, step):
        field, new = stress_field(sys, step), vel_field(sys, step)
        parcel = wraps(sys, 2 * step, STRESS_AHEAD)
        for r in range(NRAD):
            inv_s, inv_c, inv_sa, inv_ca = [geo[i, r] for i in range(4)]
            if step == 0:
                old = [raw[sys, c, rows(r)] for c in range(3)]
            else:
                old = [vel[sys, 0, c, R0 + r, LO:HI] for c in range(3)]
            s_rr, s_tt = field[RR, R0 + r, LO:HI], field[TT, R0 + r, LO:HI]
            s_rt, s_rz = field[RT, R0 + r, LO:HI], field[RZ, R0 + r, LO:HI]
            push = [
                forward4(*rad4(field, RR, r, -1)) + backward4(*az4(field, RT, r, -2)) * inv_sa
                + depth_diff(sys, parcel, 0, r) + (s_rr - s_tt) * inv_s,
                backward4(*rad4(field, RT, r, -2)) + forward4(*az4(field, TT, r, -1)) * inv_ca
                + depth_diff(sys, parcel, 1, r) + 2.0 * s_rt * inv_c,
                backward4(*rad4(field, RZ, r, -2)) + backward4(*az4(field, TZ, r, -2)) * inv_ca
                + depth_diff(sys, parcel, 2, r) + s_rz * inv_c,
            ]
            gain = mat[0, r]
            for c in range(3):
                new[c, R0 + r, LO:HI] = old[c] + gain * (push[c] + inj[sys, step, c, r])

    def strain_at(sys, step, parcel, r):
        field = vel_field(sys, step)
        inv_s, inv_c, inv_sa, inv_ca = [geo[i, r] for i in range(4)]
        v_r, v_t = field[0, R0 + r, LO:HI], field[1, R0 + r, LO:HI]
        return [
            backward4(*rad4(field, 0, r, -2)),
            backward4(*az4(field, 1, r, -2)) * inv_ca + v_r * inv_c,
            depth_diff(sys, parcel, 0, r),
            0.5 * (forward4(*rad4(field, 1, r, -1)) + forward4(*az4(field, 0, r, -1)) * inv_sa
                   - v_t * inv_s),
            0.5 * (depth_diff(sys, parcel, 1, r) + forward4(*rad4(field, 2, r, -1))),
            0.5 * (depth_diff(sys, parcel, 2, r) + forward4(*az4(field, 2, r, -1)) * inv_ca),
        ]

    def load_state(sys):
        got_stress[sys].wait()
        field = stress_field(sys, 0)
        for c in range(6):
            for r in range(NRAD):
                field[c, R0 + r, LO:HI] = raw[sys, IN_STATE[c], rows(r)]

    load_state(ADJ)
    pl.semaphore_wait(barrier, 3 + has_up.astype(jnp.int32) + has_dn.astype(jnp.int32))
    legs_s = [None, None]
    legs_v = [None, None]
    legs_s[ADJ] = send_stress(ADJ, 0)
    load_state(FWD)
    legs_s[FWD] = send_stress(FWD, 0)

    @pl.when(rad == 0)
    def _():
        for sys in (ADJ, FWD):
            for step in range(2):
                stress[sys, step, 0:3, 0:R0, LO:HI] = jnp.zeros((3, R0, NAZ, LANES), f32)
                vel[sys, step, :, 0:R0, LO:HI] = jnp.zeros((3, R0, NAZ, LANES), f32)

    @pl.when(rad == n_rad - 1)
    def _():
        for sys in (ADJ, FWD):
            for step in range(2):
                stress[sys, step, 0:3, R0 + NRAD:, LO:HI] = jnp.zeros((3, 2, NAZ, LANES), f32)
                vel[sys, step, :, R0 + NRAD:, LO:HI] = jnp.zeros((3, 2, NAZ, LANES), f32)

    for copy in got_small:
        copy.wait()
    angle = 2.0 * math.pi / (NAZ * n_az)
    inner = (NAZ * n_az) / (2.0 * math.pi)
    for r in range(NRAD):
        centre = jnp.full((NAZ, LANES), f32(inner), f32) + (rad * NRAD + r).astype(f32)
        staggered = centre + 0.5
        geo[0, r] = 1.0 / staggered
        geo[1, r] = 1.0 / centre
        geo[2, r] = 1.0 / (staggered * angle)
        geo[3, r] = 1.0 / (centre * angle)

    betas = []
    for r in range(NRAD):
        zone = zone_v[rows(r)]
        looked = [jnp.zeros((NAZ, LANES), f32) for _ in range(8)]
        for number in range(8):
            hit = zone == number
            for t in range(8):
                ref, row = (ze, t) if t < 2 else (zr, t - 2) if t < 5 else (zw, t - 5)
                looked[t] = jnp.where(hit, ref[row, number], looked[t])
        lame, buoyancy = looked[0], looked[1]
        alpha = [DT * looked[2 + i] for i in range(3)]
        weight = looked[5:8]
        beta = [1.0 - a for a in alpha]
        share = [a * w for a, w in zip(alpha, weight)]
        gain = DT * (1.0 - (share[0] + share[1] + share[2]))
        later = DT * (beta[0] * share[0] + beta[1] * share[1] + beta[2] * share[2])
        doubled = 2.0 * mu_v[rows(r)]
        mat[0, r] = DT * buoyancy
        mat[1, r] = gain * lame
        mat[2, r] = gain * doubled
        mat[3, r] = later * lame
        mat[4, r] = later * doubled
        for i in range(3):
            mat[5 + i, r] = beta[i]

    def inject(sys, cells_ref, force_ref, count):
        cells = cells_ref[...]
        around = lax.shift_right_logical(cells, 13) - NAZ * az
        radial = (lax.shift_right_logical(cells, 8) & 31) - NRAD * rad
        depth = (cells & 255) - LANES * dep
        inside = (around >= 0) & (around < NAZ) & (radial >= 0) & (radial < NRAD)
        key = jnp.where(inside, radial * NAZ + around, -1)
        here = lax.broadcasted_iota(jnp.int32, (NRAD * NAZ, count), 0) == key
        lanes = (lax.broadcasted_iota(jnp.int32, (LANES, count), 0) == depth).astype(f32)
        for step in range(2):
            for c in range(3):
                picked = jnp.where(here, force_ref[c, step: step + 1, :], 0.0)
                total = lax.dot_general(
                    picked, lanes, (((1,), (1,)), ((), ())),
                    precision=lax.Precision.HIGHEST, preferred_element_type=f32,
                )
                for r in range(NRAD):
                    inj[sys, step, c, r] = total[r * NAZ: (r + 1) * NAZ]

    inject(ADJ, rc_v, rr_v, rc_v.shape[1])
    inject(FWD, sc_v, sf_v, sc_v.shape[1])
    for sys in (ADJ, FWD):
        got_vel[sys].wait()

    def advance_velocity(sys, step):
        arrive(legs_s[sys])
        velocity_update(sys, step)
        legs_v[sys] = send_vel(sys, step)

    for sys in (ADJ, FWD):
        advance_velocity(sys, 0)

    for sys in (ADJ, FWD):
        got_mem[sys].wait()
        for r in range(NRAD):
            beta = [mat[5 + i, r] for i in range(3)]
            for e in range(6):
                m = [beta[i] * mem[sys, 6 * i + e, rows(r)] for i in range(3)]
                a1[sys, e, r] = raw[sys, 3 + e, rows(r)] - DT * (m[0] + m[1] + m[2])
                if sys == ADJ:
                    a2[e, r] = DT * (beta[0] * m[0] + beta[1] * m[1] + beta[2] * m[2])

    def first_stress(sys):
        arrive(legs_v[sys])
        parcel = wraps(sys, 1, VEL_AHEAD)
        new = stress_field(sys, 1)
        for r in range(NRAD):
            e = strain_at(sys, 0, parcel, r)
            dilation = e[0] + e[1] + e[2]
            common = mat[1, r] * dilation
            gm = mat[2, r]
            for i in range(6):
                strain[sys, 0, i, r] = e[i]
                change = gm * e[i] + common if i < 3 else gm * e[i]
                new[STRAIN_ORDER[i], R0 + r, LO:HI] = a1[sys, i, r] + change
        legs_s[sys] = send_stress(sys, 1)

    for sys in (ADJ, FWD):
        first_stress(sys)

    for r in range(NRAD):
        e = [strain[ADJ, 0, i, r] for i in range(6)]
        common = mat[3, r] * (e[0] + e[1] + e[2])
        hm = mat[4, r]
        for i in range(6):
            drop = hm * e[i] + common if i < 3 else hm * e[i]
            a2[i, r] = stress[ADJ, 1, STRAIN_ORDER[i], R0 + r, LO:HI] - a2[i, r] - drop

    for sys in (ADJ, FWD):
        advance_velocity(sys, 1)
    for r in range(NRAD):
        for c in range(3):
            out_v[c, rows(r)] = vel[ADJ, 1, c, R0 + r, LO:HI]
    out_vel = pltpu.make_async_copy(out_v.at[pl.ds(0, 3)], adj_h.at[pl.ds(0, 3)], out_sem.at[0])
    out_vel.start()

    def product(e, f):
        return 2.0 * DT * (e[0] * f[0] + e[1] * f[1] + e[2] * f[2]
                           + 2.0 * (e[3] * f[3] + e[4] * f[4] + e[5] * f[5]))

    arrive(legs_v[ADJ])
    parcel = wraps(ADJ, 3, VEL_AHEAD)
    for r in range(NRAD):
        e = strain_at(ADJ, 1, parcel, r)
        common = mat[1, r] * (e[0] + e[1] + e[2])
        gm = mat[2, r]
        for i in range(6):
            change = gm * e[i] + common if i < 3 else gm * e[i]
            out_v[3 + i, rows(r)] = a2[i, r] + change
        a1[ADJ, 0, r] = product(e, [strain[FWD, 0, i, r] for i in range(6)])
    out_stress = pltpu.make_async_copy(out_v.at[pl.ds(3, 6)], adj_h.at[pl.ds(3, 6)], out_sem.at[1])
    out_stress.start()

    arrive(legs_v[FWD])
    parcel = wraps(FWD, 3, VEL_AHEAD)
    for r in range(NRAD):
        e = strain_at(FWD, 1, parcel, r)
        grad_v[rows(r)] = a1[ADJ, 0, r] + product(e, [strain[ADJ, 0, i, r] for i in range(6)])
    out_grad = pltpu.make_async_copy(grad_v, grad_h, out_sem.at[2])
    out_grad.start()

    for legs, up_legs, dn_legs in started:
        for make in legs:
            make().wait_send()

    @pl.when(has_up)
    def _():
        for _, up_legs, _ in started:
            for make in up_legs:
                make().wait_send()

    @pl.when(has_dn)
    def _():
        for _, _, dn_legs in started:
            for make in dn_legs:
                make().wait_send()

    out_vel.wait()
    out_stress.wait()
    out_grad.wait()


def hand_on(grad_in, adj_in, grad_out, adj_out, sems):
    copies = [
        pltpu.make_async_copy(adj_in.at[pl.ds(3 * i, 3)], adj_out.at[pl.ds(3 * i, 3)], sems.at[i])
        for i in range(3)
    ] + [pltpu.make_async_copy(grad_in, grad_out, sems.at[3])]
    for copy in copies:
        copy.start()
    for copy in copies:
        copy.wait()


def shards(
    forward_state, forward_memory, adjoint_state, adjoint_memory, shear_modulus, zone,
    zone_elastic, zone_rates, zone_weights, source_cells, source_force, receiver_cells,
    receiver_residual,
):
    cells = NAZ * NRAD
    nsrc, nrec = source_cells.shape[0], receiver_cells.shape[0]
    block = (NRAD, NAZ, LANES)
    vmem = pltpu.VMEM
    hbm = pl.BlockSpec(memory_space=pltpu.HBM)
    gradient, adjoint_out = pl.pallas_call(
        kernel,
        out_shape=(
            jax.ShapeDtypeStruct((cells, LANES), f32),
            jax.ShapeDtypeStruct((9, cells, LANES), f32),
        ),
        in_specs=[hbm] * 13,
        out_specs=(hbm, hbm),
        scratch_shapes=[
            vmem((2, 9, cells, LANES), f32),
            vmem((2, 18, cells, LANES), f32),
            vmem((cells, LANES), f32),
            vmem((cells, LANES), jnp.int32),
            pltpu.SMEM((2, 8), f32),
            pltpu.SMEM((3, 8), f32),
            pltpu.SMEM((3, 8), f32),
            vmem((1, nsrc), jnp.int32),
            vmem((3, 2, nsrc), f32),
            vmem((1, nrec), jnp.int32),
            vmem((3, 2, nrec), f32),
            vmem((2, 2, 6, NRAD + 4, NAZ + 16, LANES), f32),
            vmem((2, 2, 3, NRAD + 4, NAZ + 16, LANES), f32),
            vmem((2, 3) + block, f32),
            vmem((2, 4, 8, LANES), f32),
            vmem((2, 4, 8, LANES), f32),
            vmem((2, 1, 6) + block, f32),
            vmem((2, 6) + block, f32),
            vmem((6,) + block, f32),
            vmem((2, 2, 3) + block, f32),
            vmem((4,) + block, f32),
            vmem((8,) + block, f32),
            vmem((9, cells, LANES), f32),
            vmem((cells, LANES), f32),
            pltpu.SemaphoreType.DMA((16,)),
            pltpu.SemaphoreType.DMA((3,)),
            pltpu.SemaphoreType.DMA((2, 4, 7)),
            pltpu.SemaphoreType.DMA((2, 4, 7)),
        ],
        compiler_params=pltpu.CompilerParams(
            collective_id=0, has_side_effects=True, vmem_limit_bytes=60 * 2**20
        ),
        name="window",
    )(
        forward_state.reshape(9, cells, LANES),
        forward_memory.reshape(18, cells, LANES),
        adjoint_state.reshape(9, cells, LANES),
        adjoint_memory.reshape(18, cells, LANES),
        shear_modulus.reshape(cells, LANES),
        zone.reshape(cells, LANES),
        zone_elastic, zone_rates, zone_weights,
        source_cells.reshape(1, nsrc), source_force.transpose(1, 0, 2),
        receiver_cells.reshape(1, nrec), receiver_residual.transpose(1, 0, 2),
    )
    gradient, adjoint_out = pl.pallas_call(
        hand_on,
        out_shape=(
            jax.ShapeDtypeStruct((cells, LANES), f32),
            jax.ShapeDtypeStruct((9, cells, LANES), f32),
        ),
        in_specs=[hbm, hbm],
        out_specs=(hbm, hbm),
        scratch_shapes=[pltpu.SemaphoreType.DMA((4,))],
        compiler_params=pltpu.CompilerParams(vmem_limit_bytes=60 * 2**20),
        name="hand_on",
    )(gradient, adjoint_out)
    return gradient.reshape(NAZ, NRAD, LANES), adjoint_out.reshape(9, NAZ, NRAD, LANES)


def solution(mesh):
    return jax.shard_map(
        shards,
        mesh=mesh,
        in_specs=(
            P(None, "az", "rad", "dep"),
            P(None, None, "az", "rad", "dep"),
            P(None, "az", "rad", "dep"),
            P(None, None, "az", "rad", "dep"),
            P("az", "rad", "dep"),
            P("az", "rad", "dep"),
            P(), P(), P(), P(), P(), P(), P(),
        ),
        out_specs=(P("az", "rad", "dep"), P(None, "az", "rad", "dep")),
        check_vma=False,
    )
```

```python
import math

import jax
import jax.numpy as jnp
from jax import lax
from jax.experimental import pallas as pl
from jax.experimental.pallas import tpu as pltpu
from jax.sharding import PartitionSpec as P

MESH = pl.DeviceIdType.MESH
f32 = jnp.float32

DT = 0.2
C1 = 1.125
C2 = 1.0 / 24.0

RR, RZ, RT, TT, TZ, ZZ = range(6)
IN_STATE = {RR: 3, TT: 4, ZZ: 5, RT: 6, RZ: 7, TZ: 8}
STRAIN_ORDER = (RR, TT, ZZ, RT, RZ, TZ)

ADJ, FWD = 0, 1
NAZ, NRAD, LANES = 16, 4, 128
LO, HI = 8, 8 + NAZ
R0 = 2


class View:
    def __init__(self, ref, sys, step):
        self.ref, self.lead = ref, (sys, step)

    def __getitem__(self, index):
        return self.ref[self.lead + index]

    def __setitem__(self, index, value):
        self.ref[self.lead + index] = value

    def slab(self, index):
        return self.ref.at[self.lead + index]


def forward4(before, here, after, after2):
    return C1 * (after - here) - C2 * (after2 - before)


def backward4(before2, before, here, after):
    return C1 * (here - before) - C2 * (after - before2)


def kernel(
    fs, fm, as_, am, mu_h, zone_h, ze_h, zr_h, zw_h, sc_h, sf_h, rc_h, rr_h,
    grad_v, out_v,
    raw, mem, mu_v, zone_v, ze, zr, zw, sc_v, sf_v, rc_v, rr_v,
    stress, vel, dz, msg_out, msg_in, strain, a1, a2, inj, geo, mat,
    in_sem, send_sem, recv_sem,
):
    n_az, n_rad, n_dep = lax.axis_size("az"), lax.axis_size("rad"), lax.axis_size("dep")
    az, rad, dep = lax.axis_index("az"), lax.axis_index("rad"), lax.axis_index("dep")
    az_up, az_dn = {"az": lax.rem(az + 1, n_az)}, {"az": lax.rem(az + n_az - 1, n_az)}
    rad_up, rad_dn = {"rad": rad + 1}, {"rad": rad - 1}
    dep_other = {"dep": 1 - dep}

    has_dn, has_up = rad > 0, rad < n_rad - 1
    barrier = pltpu.get_barrier_semaphore()
    for place in (az_up, az_dn, dep_other):
        pl.semaphore_signal(barrier, inc=1, device_id=place, device_id_type=MESH)

    @pl.when(has_up)
    def _():
        pl.semaphore_signal(barrier, inc=1, device_id=rad_up, device_id_type=MESH)

    @pl.when(has_dn)
    def _():
        pl.semaphore_signal(barrier, inc=1, device_id=rad_dn, device_id_type=MESH)

    pending = []

    def bring(src, dst):
        copy = pltpu.make_async_copy(src, dst, in_sem.at[len(pending)])
        copy.start()
        pending.append(copy)
        return copy

    states = (as_, fs)
    memories = (am, fm)
    got_stress = [bring(states[s].at[pl.ds(3, 6)], raw.at[s, pl.ds(3, 6)]) for s in (ADJ, FWD)]

    got_small = [
        bring(a, b)
        for a, b in (
            (ze_h, ze), (zr_h, zr), (zw_h, zw), (sc_h, sc_v), (sf_h, sf_v), (rc_h, rc_v),
            (rr_h, rr_v), (zone_h, zone_v), (mu_h, mu_v),
        )
    ]
    got_vel = [bring(states[s].at[pl.ds(0, 3)], raw.at[s, pl.ds(0, 3)]) for s in (ADJ, FWD)]
    got_mem = [bring(memories[s], mem.at[s]) for s in (ADJ, FWD)]

    lane = lax.broadcasted_iota(jnp.int32, (NAZ, LANES), 1)
    lane8 = lax.broadcasted_iota(jnp.int32, (8, LANES), 1)

    def where_f(cond, value):
        return jnp.where(cond, f32(value), f32(0.0))

    def base(t, r, half):
        return 12 * (2 * r + half) + 4 * t

    ends = (lane8 < 2) | (lane8 >= 126)

    def pack_depth(sys, phase, gets):
        parcel = None
        for r in range(NRAD):
            for t, get in enumerate(gets):
                g = get(r)
                for half in range(2):
                    piece = jnp.where(ends, g[8 * half: 8 * half + 8], 0.0)
                    if base(t, r, half):
                        piece = pltpu.roll(piece, base(t, r, half), 1)
                    parcel = piece if parcel is None else parcel + piece
        msg_out[sys, phase] = parcel

    def local_depth(sys, gets, aheads):
        for t in range(3):
            for r in range(NRAD):
                g = gets[t](r)
                m1 = pltpu.roll(g, LANES - 1, 1)
                r1 = pltpu.roll(g, 1, 1)
                if aheads[t]:
                    m2 = pltpu.roll(g, LANES - 2, 1)
                    dz[sys, t, r] = (where_f(lane < 127, C1) * m1 - C1 * g - where_f(lane < 126, C2) * m2
                                     + where_f(lane >= 1, C2) * r1)
                else:
                    r2 = pltpu.roll(g, 2, 1)
                    dz[sys, t, r] = (C1 * g - where_f(lane >= 1, C1) * r1 - where_f(lane < 127, C2) * m1
                                     + where_f(lane >= 2, C2) * r2)

    slot = lax.rem(lax.rem(lane8 + 2, LANES), 12)
    place_in = lax.rem(slot, 4)
    which = lax.div(slot, 4)

    def wraps(sys, phase, aheads):
        x = msg_in[sys, phase]
        ahead = None
        for t in range(3):
            if aheads[t]:
                ahead = (which == t) if ahead is None else ahead | (which == t)
        behind = jnp.logical_not(ahead)
        m1, m2 = pltpu.roll(x, LANES - 1, 1), pltpu.roll(x, LANES - 2, 1)
        r1, r2 = pltpu.roll(x, 1, 1), pltpu.roll(x, 2, 1)
        at126, at127, at0, at1 = [place_in == i for i in range(4)]
        k_m1 = jnp.where(at127, jnp.where(ahead, f32(C1), f32(-C2)), 0.0)
        k_m2 = where_f(ahead & (at126 | at127), -C2)
        k_r1 = jnp.where(at0, jnp.where(ahead, f32(C2), f32(-C1)), 0.0)
        k_r2 = where_f(behind & (at0 | at1), C2)
        return k_m1 * m1 + k_m2 * m2 + k_r1 * r1 + k_r2 * r2

    mine = lane8 - 126 * (1 - dep)
    edge = (mine >= 0) & (mine < 2)

    def depth_diff(sys, parcel, t, r):
        halves = []
        for half in range(2):
            shift = base(t, r, half)
            piece = pltpu.roll(parcel, LANES - shift, 1) if shift else parcel
            halves.append(jnp.where(edge, piece, 0.0))
        return dz[sys, t, r] + jnp.concatenate(halves, axis=0)

    own = pl.ds(LO, NAZ)
    own_r = pl.ds(R0, NRAD)
    started = []

    def exchange(sys, phase, field, rad_plan, az_from, az_count):
        number = [0]
        legs, up_legs, dn_legs = [], [], []

        def leg(where, src, dst, place, group):
            n = number[0]
            number[0] += 1

            def make():
                return pltpu.make_async_remote_copy(
                    src_ref=where.slab(src), dst_ref=where.slab(dst),
                    send_sem=send_sem.at[sys, phase, n], recv_sem=recv_sem.at[sys, phase, n],
                    device_id=place, device_id_type=MESH,
                )

            make().start()
            group.append(make)

        @pl.when(has_up)
        def _():
            for first, count, up, down in rad_plan:
                comps = pl.ds(first, count)
                leg(field, (comps, pl.ds(R0 + NRAD - up, up), own), (comps, pl.ds(R0 - up, up), own),
                    rad_up, up_legs)

        @pl.when(has_dn)
        def _():
            for first, count, up, down in rad_plan:
                comps = pl.ds(first, count)
                leg(field, (comps, pl.ds(R0, down), own), (comps, pl.ds(R0 + NRAD, down), own),
                    rad_dn, dn_legs)

        comps = pl.ds(az_from, az_count)
        leg(field, (comps, own_r, pl.ds(HI - 8, 8)), (comps, own_r, pl.ds(0, 8)), az_up, legs)
        leg(field, (comps, own_r, pl.ds(LO, 8)), (comps, own_r, pl.ds(HI, 8)), az_dn, legs)
        legs_msg = number[0]

        def make_depth():
            return pltpu.make_async_remote_copy(
                src_ref=msg_out.at[sys, phase], dst_ref=msg_in.at[sys, phase],
                send_sem=send_sem.at[sys, phase, legs_msg], recv_sem=recv_sem.at[sys, phase, legs_msg],
                device_id=dep_other, device_id_type=MESH,
            )

        make_depth().start()
        legs.append(make_depth)
        groups = legs, up_legs, dn_legs
        started.append(groups)
        return groups

    def arrive(groups):
        legs, up_legs, dn_legs = groups
        for make in legs:
            make().wait_recv()

        @pl.when(has_dn)
        def _():
            for make in up_legs:
                make().wait_recv()

        @pl.when(has_up)
        def _():
            for make in dn_legs:
                make().wait_recv()

    def rows(r):
        return pl.ds(r, NAZ, stride=NRAD)

    def stress_field(sys, step):
        return View(stress, sys, step)

    def vel_field(sys, step):
        return View(vel, sys, step)

    STRESS_AHEAD = (False, False, True)
    VEL_AHEAD = (False, True, True)

    def send_stress(sys, step):
        field = stress_field(sys, step)
        gets = [lambda r, c=c: field[c, R0 + r, LO:HI] for c in (RZ, TZ, ZZ)]
        pack_depth(sys, 2 * step, gets)
        groups = exchange(sys, 2 * step, field, ((RR, 1, 1, 2), (RZ, 2, 2, 1)), RT, 3)
        local_depth(sys, gets, STRESS_AHEAD)
        return groups

    def send_vel(sys, step):
        field = vel_field(sys, step)
        gets = [lambda r, c=c: field[c, R0 + r, LO:HI] for c in (2, 0, 1)]
        pack_depth(sys, 2 * step + 1, gets)
        groups = exchange(sys, 2 * step + 1, field, ((0, 1, 2, 1), (1, 2, 1, 2)), 0, 3)
        local_depth(sys, gets, VEL_AHEAD)
        return groups

    def rad4(field, c, r, first):
        return [field[c, R0 + r + first + i, LO:HI] for i in range(4)]

    def az4(field, c, r, first):
        return [field[c, R0 + r, LO + first + i: HI + first + i] for i in range(4)]

    def velocity_update(sys, step):
        field, new = stress_field(sys, step), vel_field(sys, step)
        parcel = wraps(sys, 2 * step, STRESS_AHEAD)
        for r in range(NRAD):
            inv_s, inv_c, inv_sa, inv_ca = [geo[i, r] for i in range(4)]
            if step == 0:
                old = [raw[sys, c, rows(r)] for c in range(3)]
            else:
                old = [vel[sys, 0, c, R0 + r, LO:HI] for c in range(3)]
            s_rr, s_tt = field[RR, R0 + r, LO:HI], field[TT, R0 + r, LO:HI]
            s_rt, s_rz = field[RT, R0 + r, LO:HI], field[RZ, R0 + r, LO:HI]
            push = [
                forward4(*rad4(field, RR, r, -1)) + backward4(*az4(field, RT, r, -2)) * inv_sa
                + depth_diff(sys, parcel, 0, r) + (s_rr - s_tt) * inv_s,
                backward4(*rad4(field, RT, r, -2)) + forward4(*az4(field, TT, r, -1)) * inv_ca
                + depth_diff(sys, parcel, 1, r) + 2.0 * s_rt * inv_c,
                backward4(*rad4(field, RZ, r, -2)) + backward4(*az4(field, TZ, r, -2)) * inv_ca
                + depth_diff(sys, parcel, 2, r) + s_rz * inv_c,
            ]
            gain = mat[0, r]
            for c in range(3):
                new[c, R0 + r, LO:HI] = old[c] + gain * (push[c] + inj[sys, step, c, r])

    def strain_at(sys, step, parcel, r):
        field = vel_field(sys, step)
        inv_s, inv_c, inv_sa, inv_ca = [geo[i, r] for i in range(4)]
        v_r, v_t = field[0, R0 + r, LO:HI], field[1, R0 + r, LO:HI]
        return [
            backward4(*rad4(field, 0, r, -2)),
            backward4(*az4(field, 1, r, -2)) * inv_ca + v_r * inv_c,
            depth_diff(sys, parcel, 0, r),
            0.5 * (forward4(*rad4(field, 1, r, -1)) + forward4(*az4(field, 0, r, -1)) * inv_sa
                   - v_t * inv_s),
            0.5 * (depth_diff(sys, parcel, 1, r) + forward4(*rad4(field, 2, r, -1))),
            0.5 * (depth_diff(sys, parcel, 2, r) + forward4(*az4(field, 2, r, -1)) * inv_ca),
        ]

    def load_state(sys):
        got_stress[sys].wait()
        field = stress_field(sys, 0)
        for c in range(6):
            for r in range(NRAD):
                field[c, R0 + r, LO:HI] = raw[sys, IN_STATE[c], rows(r)]

    load_state(ADJ)
    pl.semaphore_wait(barrier, 3 + has_up.astype(jnp.int32) + has_dn.astype(jnp.int32))
    legs_s = [None, None]
    legs_v = [None, None]
    legs_s[ADJ] = send_stress(ADJ, 0)
    load_state(FWD)
    legs_s[FWD] = send_stress(FWD, 0)

    @pl.when(rad == 0)
    def _():
        for sys in (ADJ, FWD):
            for step in range(2):
                stress[sys, step, 0:3, 0:R0, LO:HI] = jnp.zeros((3, R0, NAZ, LANES), f32)
                vel[sys, step, :, 0:R0, LO:HI] = jnp.zeros((3, R0, NAZ, LANES), f32)

    @pl.when(rad == n_rad - 1)
    def _():
        for sys in (ADJ, FWD):
            for step in range(2):
                stress[sys, step, 0:3, R0 + NRAD:, LO:HI] = jnp.zeros((3, 2, NAZ, LANES), f32)
                vel[sys, step, :, R0 + NRAD:, LO:HI] = jnp.zeros((3, 2, NAZ, LANES), f32)

    for copy in got_small:
        copy.wait()
    angle = 2.0 * math.pi / (NAZ * n_az)
    inner = (NAZ * n_az) / (2.0 * math.pi)
    for r in range(NRAD):
        centre = jnp.full((NAZ, LANES), f32(inner), f32) + (rad * NRAD + r).astype(f32)
        staggered = centre + 0.5
        geo[0, r] = 1.0 / staggered
        geo[1, r] = 1.0 / centre
        geo[2, r] = 1.0 / (staggered * angle)
        geo[3, r] = 1.0 / (centre * angle)

    betas = []
    for r in range(NRAD):
        zone = zone_v[rows(r)]
        looked = [jnp.zeros((NAZ, LANES), f32) for _ in range(8)]
        for number in range(8):
            hit = zone == number
            for t in range(8):
                ref, row = (ze, t) if t < 2 else (zr, t - 2) if t < 5 else (zw, t - 5)
                looked[t] = jnp.where(hit, ref[row, number], looked[t])
        lame, buoyancy = looked[0], looked[1]
        alpha = [DT * looked[2 + i] for i in range(3)]
        weight = looked[5:8]
        beta = [1.0 - a for a in alpha]
        share = [a * w for a, w in zip(alpha, weight)]
        gain = DT * (1.0 - (share[0] + share[1] + share[2]))
        later = DT * (beta[0] * share[0] + beta[1] * share[1] + beta[2] * share[2])
        doubled = 2.0 * mu_v[rows(r)]
        mat[0, r] = DT * buoyancy
        mat[1, r] = gain * lame
        mat[2, r] = gain * doubled
        mat[3, r] = later * lame
        mat[4, r] = later * doubled
        for i in range(3):
            mat[5 + i, r] = beta[i]

    def inject(sys, cells_ref, force_ref, count):
        cells = cells_ref[...]
        around = lax.shift_right_logical(cells, 13) - NAZ * az
        radial = (lax.shift_right_logical(cells, 8) & 31) - NRAD * rad
        depth = (cells & 255) - LANES * dep
        inside = (around >= 0) & (around < NAZ) & (radial >= 0) & (radial < NRAD)
        key = jnp.where(inside, radial * NAZ + around, -1)
        here = lax.broadcasted_iota(jnp.int32, (NRAD * NAZ, count), 0) == key
        lanes = (lax.broadcasted_iota(jnp.int32, (LANES, count), 0) == depth).astype(f32)
        for step in range(2):
            for c in range(3):
                picked = jnp.where(here, force_ref[c, step: step + 1, :], 0.0)
                total = lax.dot_general(
                    picked, lanes, (((1,), (1,)), ((), ())),
                    precision=lax.Precision.HIGHEST, preferred_element_type=f32,
                )
                for r in range(NRAD):
                    inj[sys, step, c, r] = total[r * NAZ: (r + 1) * NAZ]

    inject(ADJ, rc_v, rr_v, rc_v.shape[1])
    inject(FWD, sc_v, sf_v, sc_v.shape[1])
    for sys in (ADJ, FWD):
        got_vel[sys].wait()

    def advance_velocity(sys, step):
        arrive(legs_s[sys])
        velocity_update(sys, step)
        legs_v[sys] = send_vel(sys, step)

    for sys in (ADJ, FWD):
        advance_velocity(sys, 0)

    for sys in (ADJ, FWD):
        got_mem[sys].wait()
        for r in range(NRAD):
            beta = [mat[5 + i, r] for i in range(3)]
            for e in range(6):
                m = [beta[i] * mem[sys, 6 * i + e, rows(r)] for i in range(3)]
                a1[sys, e, r] = raw[sys, 3 + e, rows(r)] - DT * (m[0] + m[1] + m[2])
                if sys == ADJ:
                    a2[e, r] = DT * (beta[0] * m[0] + beta[1] * m[1] + beta[2] * m[2])

    def first_stress(sys):
        arrive(legs_v[sys])
        parcel = wraps(sys, 1, VEL_AHEAD)
        new = stress_field(sys, 1)
        for r in range(NRAD):
            e = strain_at(sys, 0, parcel, r)
            dilation = e[0] + e[1] + e[2]
            common = mat[1, r] * dilation
            gm = mat[2, r]
            for i in range(6):
                strain[sys, 0, i, r] = e[i]
                change = gm * e[i] + common if i < 3 else gm * e[i]
                new[STRAIN_ORDER[i], R0 + r, LO:HI] = a1[sys, i, r] + change
        legs_s[sys] = send_stress(sys, 1)

    for sys in (ADJ, FWD):
        first_stress(sys)

    for r in range(NRAD):
        e = [strain[ADJ, 0, i, r] for i in range(6)]
        common = mat[3, r] * (e[0] + e[1] + e[2])
        hm = mat[4, r]
        for i in range(6):
            drop = hm * e[i] + common if i < 3 else hm * e[i]
            a2[i, r] = stress[ADJ, 1, STRAIN_ORDER[i], R0 + r, LO:HI] - a2[i, r] - drop

    for sys in (ADJ, FWD):
        advance_velocity(sys, 1)
    for r in range(NRAD):
        for c in range(3):
            out_v[c, rows(r)] = vel[ADJ, 1, c, R0 + r, LO:HI]

    def product(e, f):
        return 2.0 * DT * (e[0] * f[0] + e[1] * f[1] + e[2] * f[2]
                           + 2.0 * (e[3] * f[3] + e[4] * f[4] + e[5] * f[5]))

    arrive(legs_v[ADJ])
    parcel = wraps(ADJ, 3, VEL_AHEAD)
    for r in range(NRAD):
        e = strain_at(ADJ, 1, parcel, r)
        common = mat[1, r] * (e[0] + e[1] + e[2])
        gm = mat[2, r]
        for i in range(6):
            change = gm * e[i] + common if i < 3 else gm * e[i]
            out_v[3 + i, rows(r)] = a2[i, r] + change
        a1[ADJ, 0, r] = product(e, [strain[FWD, 0, i, r] for i in range(6)])

    arrive(legs_v[FWD])
    parcel = wraps(FWD, 3, VEL_AHEAD)
    for r in range(NRAD):
        e = strain_at(FWD, 1, parcel, r)
        grad_v[rows(r)] = a1[ADJ, 0, r] + product(e, [strain[ADJ, 0, i, r] for i in range(6)])

    for legs, up_legs, dn_legs in started:
        for make in legs:
            make().wait_send()

    @pl.when(has_up)
    def _():
        for _, up_legs, _ in started:
            for make in up_legs:
                make().wait_send()

    @pl.when(has_dn)
    def _():
        for _, _, dn_legs in started:
            for make in dn_legs:
                make().wait_send()


def hand_on(grad_in, adj_in, grad_out, adj_out, sems):
    copies = [pltpu.make_async_copy(adj_in, adj_out, sems.at[0]),
              pltpu.make_async_copy(grad_in, grad_out, sems.at[1])]
    for copy in copies:
        copy.start()
    for copy in copies:
        copy.wait()


def shards(
    forward_state, forward_memory, adjoint_state, adjoint_memory, shear_modulus, zone,
    zone_elastic, zone_rates, zone_weights, source_cells, source_force, receiver_cells,
    receiver_residual,
):
    cells = NAZ * NRAD
    nsrc, nrec = source_cells.shape[0], receiver_cells.shape[0]
    block = (NRAD, NAZ, LANES)
    vmem = pltpu.VMEM
    hbm = pl.BlockSpec(memory_space=pltpu.HBM)
    gradient, adjoint_out = pl.pallas_call(
        kernel,
        out_shape=(vmem((cells, LANES), f32), vmem((9, cells, LANES), f32)),
        in_specs=[hbm] * 13,
        out_specs=(pl.BlockSpec(memory_space=pltpu.VMEM),) * 2,
        scratch_shapes=[
            vmem((2, 9, cells, LANES), f32),
            vmem((2, 18, cells, LANES), f32),
            vmem((cells, LANES), f32),
            vmem((cells, LANES), jnp.int32),
            pltpu.SMEM((2, 8), f32),
            pltpu.SMEM((3, 8), f32),
            pltpu.SMEM((3, 8), f32),
            vmem((1, nsrc), jnp.int32),
            vmem((3, 2, nsrc), f32),
            vmem((1, nrec), jnp.int32),
            vmem((3, 2, nrec), f32),
            vmem((2, 2, 6, NRAD + 4, NAZ + 16, LANES), f32),
            vmem((2, 2, 3, NRAD + 4, NAZ + 16, LANES), f32),
            vmem((2, 3) + block, f32),
            vmem((2, 4, 8, LANES), f32),
            vmem((2, 4, 8, LANES), f32),
            vmem((2, 1, 6) + block, f32),
            vmem((2, 6) + block, f32),
            vmem((6,) + block, f32),
            vmem((2, 2, 3) + block, f32),
            vmem((4,) + block, f32),
            vmem((8,) + block, f32),
            pltpu.SemaphoreType.DMA((16,)),
            pltpu.SemaphoreType.DMA((2, 4, 7)),
            pltpu.SemaphoreType.DMA((2, 4, 7)),
        ],
        compiler_params=pltpu.CompilerParams(
            collective_id=0, has_side_effects=True, vmem_limit_bytes=60 * 2**20
        ),
        name="window",
    )(
        forward_state.reshape(9, cells, LANES),
        forward_memory.reshape(18, cells, LANES),
        adjoint_state.reshape(9, cells, LANES),
        adjoint_memory.reshape(18, cells, LANES),
        shear_modulus.reshape(cells, LANES),
        zone.reshape(cells, LANES),
        zone_elastic, zone_rates, zone_weights,
        source_cells.reshape(1, nsrc), source_force.transpose(1, 0, 2),
        receiver_cells.reshape(1, nrec), receiver_residual.transpose(1, 0, 2),
    )
    gradient, adjoint_out = pl.pallas_call(
        hand_on,
        out_shape=(
            jax.ShapeDtypeStruct((cells, LANES), f32),
            jax.ShapeDtypeStruct((9, cells, LANES), f32),
        ),
        in_specs=[pl.BlockSpec(memory_space=pl.ANY)] * 2,
        out_specs=(hbm, hbm),
        scratch_shapes=[pltpu.SemaphoreType.DMA((2,))],
        compiler_params=pltpu.CompilerParams(vmem_limit_bytes=2**20),
        name="hand_on",
    )(gradient, adjoint_out)
    return gradient.reshape(NAZ, NRAD, LANES), adjoint_out.reshape(9, NAZ, NRAD, LANES)


def solution(mesh):
    return jax.shard_map(
        shards,
        mesh=mesh,
        in_specs=(
            P(None, "az", "rad", "dep"),
            P(None, None, "az", "rad", "dep"),
            P(None, "az", "rad", "dep"),
            P(None, None, "az", "rad", "dep"),
            P("az", "rad", "dep"),
            P("az", "rad", "dep"),
            P(), P(), P(), P(), P(), P(), P(),
        ),
        out_specs=(P("az", "rad", "dep"), P(None, "az", "rad", "dep")),
        check_vma=False,
    )
```

```python
import math

import jax
import jax.numpy as jnp
from jax import lax
from jax.experimental import pallas as pl
from jax.experimental.pallas import tpu as pltpu
from jax.sharding import PartitionSpec as P

MESH = pl.DeviceIdType.MESH
f32 = jnp.float32

DT = 0.2
C1 = 1.125
C2 = 1.0 / 24.0

RR, RZ, RT, TT, TZ, ZZ = range(6)
IN_STATE = {RR: 3, TT: 4, ZZ: 5, RT: 6, RZ: 7, TZ: 8}
STRAIN_ORDER = (RR, TT, ZZ, RT, RZ, TZ)

ADJ, FWD = 0, 1
NAZ, NRAD, LANES = 16, 4, 128
LO, HI = 8, 8 + NAZ
R0 = 2


class View:
    def __init__(self, ref, sys, step):
        self.ref, self.lead = ref, (sys, step)

    def __getitem__(self, index):
        return self.ref[self.lead + index]

    def __setitem__(self, index, value):
        self.ref[self.lead + index] = value

    def slab(self, index):
        return self.ref.at[self.lead + index]


def forward4(before, here, after, after2):
    return C1 * (after - here) - C2 * (after2 - before)


def backward4(before2, before, here, after):
    return C1 * (here - before) - C2 * (after - before2)


def kernel(
    fs, fm, as_, am, mu_h, zone_h, ze_h, zr_h, zw_h, sc_h, sf_h, rc_h, rr_h,
    grad_v, out_v,
    raw, mem, mu_v, zone_v, ze, zr, zw, sc_v, sf_v, rc_v, rr_v,
    stress, vel, dz, az_out, az_in, msg_out, msg_in, strain, a1, a2, inj, geo, mat,
    in_sem, send_sem, recv_sem,
):
    n_az, n_rad, n_dep = lax.axis_size("az"), lax.axis_size("rad"), lax.axis_size("dep")
    az, rad, dep = lax.axis_index("az"), lax.axis_index("rad"), lax.axis_index("dep")
    az_up, az_dn = {"az": lax.rem(az + 1, n_az)}, {"az": lax.rem(az + n_az - 1, n_az)}
    rad_up, rad_dn = {"rad": rad + 1}, {"rad": rad - 1}
    dep_other = {"dep": 1 - dep}

    has_dn, has_up = rad > 0, rad < n_rad - 1
    barrier = pltpu.get_barrier_semaphore()
    for place in (az_up, az_dn, dep_other):
        pl.semaphore_signal(barrier, inc=1, device_id=place, device_id_type=MESH)

    @pl.when(has_up)
    def _():
        pl.semaphore_signal(barrier, inc=1, device_id=rad_up, device_id_type=MESH)

    @pl.when(has_dn)
    def _():
        pl.semaphore_signal(barrier, inc=1, device_id=rad_dn, device_id_type=MESH)

    pending = []

    def bring(src, dst):
        copy = pltpu.make_async_copy(src, dst, in_sem.at[len(pending)])
        copy.start()
        pending.append(copy)
        return copy

    states = (as_, fs)
    memories = (am, fm)
    got_stress = [bring(states[s].at[pl.ds(3, 6)], raw.at[s, pl.ds(3, 6)]) for s in (ADJ, FWD)]

    got_small = [
        bring(a, b)
        for a, b in (
            (ze_h, ze), (zr_h, zr), (zw_h, zw), (sc_h, sc_v), (sf_h, sf_v), (rc_h, rc_v),
            (rr_h, rr_v), (zone_h, zone_v), (mu_h, mu_v),
        )
    ]
    got_vel = [bring(states[s].at[pl.ds(0, 3)], raw.at[s, pl.ds(0, 3)]) for s in (ADJ, FWD)]
    got_mem = [bring(memories[s], mem.at[s]) for s in (ADJ, FWD)]

    lane = lax.broadcasted_iota(jnp.int32, (NAZ, LANES), 1)
    lane8 = lax.broadcasted_iota(jnp.int32, (8, LANES), 1)

    def where_f(cond, value):
        return jnp.where(cond, f32(value), f32(0.0))

    def base(t, r, half):
        return 12 * (2 * r + half) + 4 * t

    ends = (lane8 < 2) | (lane8 >= 126)

    def pack_depth(sys, phase, gets):
        parcel = None
        for r in range(NRAD):
            for t, get in enumerate(gets):
                g = get(r)
                for half in range(2):
                    piece = jnp.where(ends, g[8 * half: 8 * half + 8], 0.0)
                    if base(t, r, half):
                        piece = pltpu.roll(piece, base(t, r, half), 1)
                    parcel = piece if parcel is None else parcel + piece
        msg_out[sys, phase] = parcel

    def local_depth(sys, gets, aheads):
        for t in range(3):
            for r in range(NRAD):
                g = gets[t](r)
                m1 = pltpu.roll(g, LANES - 1, 1)
                r1 = pltpu.roll(g, 1, 1)
                if aheads[t]:
                    m2 = pltpu.roll(g, LANES - 2, 1)
                    dz[sys, t, r] = (where_f(lane < 127, C1) * m1 - C1 * g - where_f(lane < 126, C2) * m2
                                     + where_f(lane >= 1, C2) * r1)
                else:
                    r2 = pltpu.roll(g, 2, 1)
                    dz[sys, t, r] = (C1 * g - where_f(lane >= 1, C1) * r1 - where_f(lane < 127, C2) * m1
                                     + where_f(lane >= 2, C2) * r2)

    slot = lax.rem(lax.rem(lane8 + 2, LANES), 12)
    place_in = lax.rem(slot, 4)
    which = lax.div(slot, 4)

    def wraps(sys, phase, aheads):
        x = msg_in[sys, phase]
        ahead = None
        for t in range(3):
            if aheads[t]:
                ahead = (which == t) if ahead is None else ahead | (which == t)
        behind = jnp.logical_not(ahead)
        m1, m2 = pltpu.roll(x, LANES - 1, 1), pltpu.roll(x, LANES - 2, 1)
        r1, r2 = pltpu.roll(x, 1, 1), pltpu.roll(x, 2, 1)
        at126, at127, at0, at1 = [place_in == i for i in range(4)]
        k_m1 = jnp.where(at127, jnp.where(ahead, f32(C1), f32(-C2)), 0.0)
        k_m2 = where_f(ahead & (at126 | at127), -C2)
        k_r1 = jnp.where(at0, jnp.where(ahead, f32(C2), f32(-C1)), 0.0)
        k_r2 = where_f(behind & (at0 | at1), C2)
        return k_m1 * m1 + k_m2 * m2 + k_r1 * r1 + k_r2 * r2

    mine = lane8 - 126 * (1 - dep)
    edge = (mine >= 0) & (mine < 2)

    def depth_diff(sys, parcel, t, r):
        halves = []
        for half in range(2):
            shift = base(t, r, half)
            piece = pltpu.roll(parcel, LANES - shift, 1) if shift else parcel
            halves.append(jnp.where(edge, piece, 0.0))
        return dz[sys, t, r] + jnp.concatenate(halves, axis=0)

    own = pl.ds(LO, NAZ)
    started = []

    def exchange(sys, phase, field, rad_plan, az_from, gets):
        number = [0]
        legs, up_legs, dn_legs = [], [], []

        def leg(src, dst, place, group):
            n = number[0]
            number[0] += 1

            def make():
                return pltpu.make_async_remote_copy(
                    src_ref=src(), dst_ref=dst(),
                    send_sem=send_sem.at[sys, phase, n], recv_sem=recv_sem.at[sys, phase, n],
                    device_id=place, device_id_type=MESH,
                )

            make().start()
            group.append(make)

        def layers(first, count, start, size):
            return lambda: field.slab((pl.ds(first, count), pl.ds(start, size), own))

        @pl.when(has_up)
        def _():
            for first, count, up, down in rad_plan:
                leg(layers(first, count, R0 + NRAD - up, up), layers(first, count, R0 - up, up),
                    rad_up, up_legs)

        @pl.when(has_dn)
        def _():
            for first, count, up, down in rad_plan:
                leg(layers(first, count, R0, down), layers(first, count, R0 + NRAD, down),
                    rad_dn, dn_legs)

        for way, row, place in ((0, HI - 2, az_up), (1, LO, az_dn)):
            for i in range(3):
                for r in range(NRAD):
                    az_out[sys, phase, way, i, 2 * r: 2 * r + 2] = field[az_from + i, R0 + r, row: row + 2]
            leg(lambda way=way: az_out.at[sys, phase, way], lambda way=way: az_in.at[sys, phase, way],
                place, legs)
        pack_depth(sys, phase, gets)
        leg(lambda: msg_out.at[sys, phase], lambda: msg_in.at[sys, phase], dep_other, legs)
        groups = legs, up_legs, dn_legs, (sys, phase, field, az_from)
        started.append(groups)
        return groups

    def arrive(groups):
        legs, up_legs, dn_legs, (sys, phase, field, az_from) = groups
        for make in legs:
            make().wait_recv()
        for way, row in ((0, LO - 2), (1, HI)):
            for i in range(3):
                for r in range(NRAD):
                    field[az_from + i, R0 + r, row: row + 2] = az_in[sys, phase, way, i, 2 * r: 2 * r + 2]

        @pl.when(has_dn)
        def _():
            for make in up_legs:
                make().wait_recv()

        @pl.when(has_up)
        def _():
            for make in dn_legs:
                make().wait_recv()

    def rows(r):
        return pl.ds(r, NAZ, stride=NRAD)

    def stress_field(sys, step):
        return View(stress, sys, step)

    def vel_field(sys, step):
        return View(vel, sys, step)

    STRESS_AHEAD = (False, False, True)
    VEL_AHEAD = (False, True, True)

    def send_stress(sys, step):
        field = stress_field(sys, step)
        gets = [lambda r, c=c: field[c, R0 + r, LO:HI] for c in (RZ, TZ, ZZ)]
        groups = exchange(sys, 2 * step, field, ((RR, 1, 1, 2), (RZ, 2, 2, 1)), RT, gets)
        local_depth(sys, gets, STRESS_AHEAD)
        return groups

    def send_vel(sys, step):
        field = vel_field(sys, step)
        gets = [lambda r, c=c: field[c, R0 + r, LO:HI] for c in (2, 0, 1)]
        groups = exchange(sys, 2 * step + 1, field, ((0, 1, 2, 1), (1, 2, 1, 2)), 0, gets)
        local_depth(sys, gets, VEL_AHEAD)
        return groups

    def rad4(field, c, r, first):
        return [field[c, R0 + r + first + i, LO:HI] for i in range(4)]

    def az4(field, c, r, first):
        return [field[c, R0 + r, LO + first + i: HI + first + i] for i in range(4)]

    def velocity_update(sys, step):
        field, new = stress_field(sys, step), vel_field(sys, step)
        parcel = wraps(sys, 2 * step, STRESS_AHEAD)
        for r in range(NRAD):
            inv_s, inv_c, inv_sa, inv_ca = [geo[i, r] for i in range(4)]
            if step == 0:
                old = [raw[sys, c, rows(r)] for c in range(3)]
            else:
                old = [vel[sys, 0, c, R0 + r, LO:HI] for c in range(3)]
            s_rr, s_tt = field[RR, R0 + r, LO:HI], field[TT, R0 + r, LO:HI]
            s_rt, s_rz = field[RT, R0 + r, LO:HI], field[RZ, R0 + r, LO:HI]
            push = [
                forward4(*rad4(field, RR, r, -1)) + backward4(*az4(field, RT, r, -2)) * inv_sa
                + depth_diff(sys, parcel, 0, r) + (s_rr - s_tt) * inv_s,
                backward4(*rad4(field, RT, r, -2)) + forward4(*az4(field, TT, r, -1)) * inv_ca
                + depth_diff(sys, parcel, 1, r) + 2.0 * s_rt * inv_c,
                backward4(*rad4(field, RZ, r, -2)) + backward4(*az4(field, TZ, r, -2)) * inv_ca
                + depth_diff(sys, parcel, 2, r) + s_rz * inv_c,
            ]
            gain = mat[0, r]
            for c in range(3):
                new[c, R0 + r, LO:HI] = old[c] + gain * (push[c] + inj[sys, step, c, r])

    def strain_at(sys, step, parcel, r):
        field = vel_field(sys, step)
        inv_s, inv_c, inv_sa, inv_ca = [geo[i, r] for i in range(4)]
        v_r, v_t = field[0, R0 + r, LO:HI], field[1, R0 + r, LO:HI]
        return [
            backward4(*rad4(field, 0, r, -2)),
            backward4(*az4(field, 1, r, -2)) * inv_ca + v_r * inv_c,
            depth_diff(sys, parcel, 0, r),
            0.5 * (forward4(*rad4(field, 1, r, -1)) + forward4(*az4(field, 0, r, -1)) * inv_sa
                   - v_t * inv_s),
            0.5 * (depth_diff(sys, parcel, 1, r) + forward4(*rad4(field, 2, r, -1))),
            0.5 * (depth_diff(sys, parcel, 2, r) + forward4(*az4(field, 2, r, -1)) * inv_ca),
        ]

    def load_state(sys):
        got_stress[sys].wait()
        field = stress_field(sys, 0)
        for c in range(6):
            for r in range(NRAD):
                field[c, R0 + r, LO:HI] = raw[sys, IN_STATE[c], rows(r)]

    load_state(ADJ)
    pl.semaphore_wait(barrier, 3 + has_up.astype(jnp.int32) + has_dn.astype(jnp.int32))
    legs_s = [None, None]
    legs_v = [None, None]
    legs_s[ADJ] = send_stress(ADJ, 0)
    load_state(FWD)
    legs_s[FWD] = send_stress(FWD, 0)

    @pl.when(rad == 0)
    def _():
        for sys in (ADJ, FWD):
            for step in range(2):
                stress[sys, step, 0:3, 0:R0, LO:HI] = jnp.zeros((3, R0, NAZ, LANES), f32)
                vel[sys, step, :, 0:R0, LO:HI] = jnp.zeros((3, R0, NAZ, LANES), f32)

    @pl.when(rad == n_rad - 1)
    def _():
        for sys in (ADJ, FWD):
            for step in range(2):
                stress[sys, step, 0:3, R0 + NRAD:, LO:HI] = jnp.zeros((3, 2, NAZ, LANES), f32)
                vel[sys, step, :, R0 + NRAD:, LO:HI] = jnp.zeros((3, 2, NAZ, LANES), f32)

    for copy in got_small:
        copy.wait()
    angle = 2.0 * math.pi / (NAZ * n_az)
    inner = (NAZ * n_az) / (2.0 * math.pi)
    for r in range(NRAD):
        centre = jnp.full((NAZ, LANES), f32(inner), f32) + (rad * NRAD + r).astype(f32)
        staggered = centre + 0.5
        geo[0, r] = 1.0 / staggered
        geo[1, r] = 1.0 / centre
        geo[2, r] = 1.0 / (staggered * angle)
        geo[3, r] = 1.0 / (centre * angle)

    betas = []
    for r in range(NRAD):
        zone = zone_v[rows(r)]
        looked = [jnp.zeros((NAZ, LANES), f32) for _ in range(8)]
        for number in range(8):
            hit = zone == number
            for t in range(8):
                ref, row = (ze, t) if t < 2 else (zr, t - 2) if t < 5 else (zw, t - 5)
                looked[t] = jnp.where(hit, ref[row, number], looked[t])
        lame, buoyancy = looked[0], looked[1]
        alpha = [DT * looked[2 + i] for i in range(3)]
        weight = looked[5:8]
        beta = [1.0 - a for a in alpha]
        share = [a * w for a, w in zip(alpha, weight)]
        gain = DT * (1.0 - (share[0] + share[1] + share[2]))
        later = DT * (beta[0] * share[0] + beta[1] * share[1] + beta[2] * share[2])
        doubled = 2.0 * mu_v[rows(r)]
        mat[0, r] = DT * buoyancy
        mat[1, r] = gain * lame
        mat[2, r] = gain * doubled
        mat[3, r] = later * lame
        mat[4, r] = later * doubled
        for i in range(3):
            mat[5 + i, r] = beta[i]

    def inject(sys, cells_ref, force_ref, count):
        cells = cells_ref[...]
        around = lax.shift_right_logical(cells, 13) - NAZ * az
        radial = (lax.shift_right_logical(cells, 8) & 31) - NRAD * rad
        depth = (cells & 255) - LANES * dep
        inside = (around >= 0) & (around < NAZ) & (radial >= 0) & (radial < NRAD)
        key = jnp.where(inside, radial * NAZ + around, -1)
        here = lax.broadcasted_iota(jnp.int32, (NRAD * NAZ, count), 0) == key
        lanes = (lax.broadcasted_iota(jnp.int32, (LANES, count), 0) == depth).astype(f32)
        for step in range(2):
            for c in range(3):
                picked = jnp.where(here, force_ref[c, step: step + 1, :], 0.0)
                total = lax.dot_general(
                    picked, lanes, (((1,), (1,)), ((), ())),
                    precision=lax.Precision.HIGHEST, preferred_element_type=f32,
                )
                for r in range(NRAD):
                    inj[sys, step, c, r] = total[r * NAZ: (r + 1) * NAZ]

    inject(ADJ, rc_v, rr_v, rc_v.shape[1])
    inject(FWD, sc_v, sf_v, sc_v.shape[1])
    for sys in (ADJ, FWD):
        got_vel[sys].wait()

    def advance_velocity(sys, step):
        arrive(legs_s[sys])
        velocity_update(sys, step)
        legs_v[sys] = send_vel(sys, step)

    for sys in (ADJ, FWD):
        advance_velocity(sys, 0)

    for sys in (ADJ, FWD):
        got_mem[sys].wait()
        for r in range(NRAD):
            beta = [mat[5 + i, r] for i in range(3)]
            for e in range(6):
                m = [beta[i] * mem[sys, 6 * i + e, rows(r)] for i in range(3)]
                a1[sys, e, r] = raw[sys, 3 + e, rows(r)] - DT * (m[0] + m[1] + m[2])
                if sys == ADJ:
                    a2[e, r] = DT * (beta[0] * m[0] + beta[1] * m[1] + beta[2] * m[2])

    def first_stress(sys):
        arrive(legs_v[sys])
        parcel = wraps(sys, 1, VEL_AHEAD)
        new = stress_field(sys, 1)
        for r in range(NRAD):
            e = strain_at(sys, 0, parcel, r)
            dilation = e[0] + e[1] + e[2]
            common = mat[1, r] * dilation
            gm = mat[2, r]
            for i in range(6):
                strain[sys, 0, i, r] = e[i]
                change = gm * e[i] + common if i < 3 else gm * e[i]
                new[STRAIN_ORDER[i], R0 + r, LO:HI] = a1[sys, i, r] + change
        legs_s[sys] = send_stress(sys, 1)

    for sys in (ADJ, FWD):
        first_stress(sys)

    for r in range(NRAD):
        e = [strain[ADJ, 0, i, r] for i in range(6)]
        common = mat[3, r] * (e[0] + e[1] + e[2])
        hm = mat[4, r]
        for i in range(6):
            drop = hm * e[i] + common if i < 3 else hm * e[i]
            a2[i, r] = stress[ADJ, 1, STRAIN_ORDER[i], R0 + r, LO:HI] - a2[i, r] - drop

    for sys in (ADJ, FWD):
        advance_velocity(sys, 1)
    for r in range(NRAD):
        for c in range(3):
            out_v[c, rows(r)] = vel[ADJ, 1, c, R0 + r, LO:HI]

    def product(e, f):
        return 2.0 * DT * (e[0] * f[0] + e[1] * f[1] + e[2] * f[2]
                           + 2.0 * (e[3] * f[3] + e[4] * f[4] + e[5] * f[5]))

    arrive(legs_v[ADJ])
    parcel = wraps(ADJ, 3, VEL_AHEAD)
    for r in range(NRAD):
        e = strain_at(ADJ, 1, parcel, r)
        common = mat[1, r] * (e[0] + e[1] + e[2])
        gm = mat[2, r]
        for i in range(6):
            change = gm * e[i] + common if i < 3 else gm * e[i]
            out_v[3 + i, rows(r)] = a2[i, r] + change
        a1[ADJ, 0, r] = product(e, [strain[FWD, 0, i, r] for i in range(6)])

    arrive(legs_v[FWD])
    parcel = wraps(FWD, 3, VEL_AHEAD)
    for r in range(NRAD):
        e = strain_at(FWD, 1, parcel, r)
        grad_v[rows(r)] = a1[ADJ, 0, r] + product(e, [strain[ADJ, 0, i, r] for i in range(6)])

    for legs, _, _, _ in started:
        for make in legs:
            make().wait_send()

    @pl.when(has_up)
    def _():
        for _, up_legs, _, _ in started:
            for make in up_legs:
                make().wait_send()

    @pl.when(has_dn)
    def _():
        for _, _, dn_legs, _ in started:
            for make in dn_legs:
                make().wait_send()


def hand_on(grad_in, adj_in, grad_out, adj_out, sems):
    copies = [pltpu.make_async_copy(adj_in, adj_out, sems.at[0]),
              pltpu.make_async_copy(grad_in, grad_out, sems.at[1])]
    for copy in copies:
        copy.start()
    for copy in copies:
        copy.wait()


def shards(
    forward_state, forward_memory, adjoint_state, adjoint_memory, shear_modulus, zone,
    zone_elastic, zone_rates, zone_weights, source_cells, source_force, receiver_cells,
    receiver_residual,
):
    cells = NAZ * NRAD
    nsrc, nrec = source_cells.shape[0], receiver_cells.shape[0]
    block = (NRAD, NAZ, LANES)
    vmem = pltpu.VMEM
    hbm = pl.BlockSpec(memory_space=pltpu.HBM)
    gradient, adjoint_out = pl.pallas_call(
        kernel,
        out_shape=(vmem((cells, LANES), f32), vmem((9, cells, LANES), f32)),
        in_specs=[hbm] * 13,
        out_specs=(pl.BlockSpec(memory_space=pltpu.VMEM),) * 2,
        scratch_shapes=[
            vmem((2, 9, cells, LANES), f32),
            vmem((2, 18, cells, LANES), f32),
            vmem((cells, LANES), f32),
            vmem((cells, LANES), jnp.int32),
            pltpu.SMEM((2, 8), f32),
            pltpu.SMEM((3, 8), f32),
            pltpu.SMEM((3, 8), f32),
            vmem((1, nsrc), jnp.int32),
            vmem((3, 2, nsrc), f32),
            vmem((1, nrec), jnp.int32),
            vmem((3, 2, nrec), f32),
            vmem((2, 2, 6, NRAD + 4, NAZ + 16, LANES), f32),
            vmem((2, 2, 3, NRAD + 4, NAZ + 16, LANES), f32),
            vmem((2, 3) + block, f32),
            vmem((2, 4, 2, 3, 8, LANES), f32),
            vmem((2, 4, 2, 3, 8, LANES), f32),
            vmem((2, 4, 8, LANES), f32),
            vmem((2, 4, 8, LANES), f32),
            vmem((2, 1, 6) + block, f32),
            vmem((2, 6) + block, f32),
            vmem((6,) + block, f32),
            vmem((2, 2, 3) + block, f32),
            vmem((4,) + block, f32),
            vmem((8,) + block, f32),
            pltpu.SemaphoreType.DMA((16,)),
            pltpu.SemaphoreType.DMA((2, 4, 7)),
            pltpu.SemaphoreType.DMA((2, 4, 7)),
        ],
        compiler_params=pltpu.CompilerParams(
            collective_id=0, has_side_effects=True, vmem_limit_bytes=60 * 2**20
        ),
        name="window",
    )(
        forward_state.reshape(9, cells, LANES),
        forward_memory.reshape(18, cells, LANES),
        adjoint_state.reshape(9, cells, LANES),
        adjoint_memory.reshape(18, cells, LANES),
        shear_modulus.reshape(cells, LANES),
        zone.reshape(cells, LANES),
        zone_elastic, zone_rates, zone_weights,
        source_cells.reshape(1, nsrc), source_force.transpose(1, 0, 2),
        receiver_cells.reshape(1, nrec), receiver_residual.transpose(1, 0, 2),
    )
    gradient, adjoint_out = pl.pallas_call(
        hand_on,
        out_shape=(
            jax.ShapeDtypeStruct((cells, LANES), f32),
            jax.ShapeDtypeStruct((9, cells, LANES), f32),
        ),
        in_specs=[pl.BlockSpec(memory_space=pl.ANY)] * 2,
        out_specs=(hbm, hbm),
        scratch_shapes=[pltpu.SemaphoreType.DMA((2,))],
        compiler_params=pltpu.CompilerParams(vmem_limit_bytes=2**20),
        name="hand_on",
    )(gradient, adjoint_out)
    return gradient.reshape(NAZ, NRAD, LANES), adjoint_out.reshape(9, NAZ, NRAD, LANES)


def solution(mesh):
    return jax.shard_map(
        shards,
        mesh=mesh,
        in_specs=(
            P(None, "az", "rad", "dep"),
            P(None, None, "az", "rad", "dep"),
            P(None, "az", "rad", "dep"),
            P(None, None, "az", "rad", "dep"),
            P("az", "rad", "dep"),
            P("az", "rad", "dep"),
            P(), P(), P(), P(), P(), P(), P(),
        ),
        out_specs=(P("az", "rad", "dep"), P(None, "az", "rad", "dep")),
        check_vma=False,
    )
```

```python
import math

import jax
import jax.numpy as jnp
from jax import lax
from jax.experimental import pallas as pl
from jax.experimental.pallas import tpu as pltpu
from jax.sharding import PartitionSpec as P

MESH = pl.DeviceIdType.MESH
f32 = jnp.float32

DT = 0.2
C1 = 1.125
C2 = 1.0 / 24.0

RR, RZ, RT, TT, TZ, ZZ = range(6)
IN_STATE = {RR: 3, TT: 4, ZZ: 5, RT: 6, RZ: 7, TZ: 8}
STRAIN_ORDER = (RR, TT, ZZ, RT, RZ, TZ)

ADJ, FWD = 0, 1
NAZ, NRAD, LANES = 16, 4, 128
LO, HI = 8, 8 + NAZ
STRESS_PLAN = (((RR, 3), (RZ, 2), (RZ, 3), (RT, 2), (RT, 3)), ((RR, 0), (RR, 1), (RZ, 0), (RT, 0)))
VEL_PLAN = (((0, 2), (0, 3), (1, 3), (2, 3)), ((0, 0), (1, 0), (1, 1), (2, 0), (2, 1)))


class View:
    def __init__(self, ref, sys, step):
        self.ref, self.lead = ref, (sys, step)

    def __getitem__(self, index):
        return self.ref[self.lead + index]

    def __setitem__(self, index, value):
        self.ref[self.lead + index] = value


def forward4(before, here, after, after2):
    return C1 * (after - here) - C2 * (after2 - before)


def backward4(before2, before, here, after):
    return C1 * (here - before) - C2 * (after - before2)


def kernel(
    fs, fm, as_, am, mu_h, zone_h, ze_h, zr_h, zw_h, sc_h, sf_h, rc_h, rr_h,
    grad_v, out_v,
    raw, mem, mu_v, zone_v, ze, zr, zw, sc_v, sf_v, rc_v, rr_v,
    stress, vel, dz, rad_out, rad_in, az_out, az_in, msg_out, msg_in, strain, a1, a2, inj, geo, mat,
    in_sem, send_sem, recv_sem,
):
    n_az, n_rad, n_dep = lax.axis_size("az"), lax.axis_size("rad"), lax.axis_size("dep")
    az, rad, dep = lax.axis_index("az"), lax.axis_index("rad"), lax.axis_index("dep")
    az_up, az_dn = {"az": lax.rem(az + 1, n_az)}, {"az": lax.rem(az + n_az - 1, n_az)}
    rad_up, rad_dn = {"rad": rad + 1}, {"rad": rad - 1}
    dep_other = {"dep": 1 - dep}

    has_dn, has_up = rad > 0, rad < n_rad - 1
    barrier = pltpu.get_barrier_semaphore()
    for place in (az_up, az_dn, dep_other):
        pl.semaphore_signal(barrier, inc=1, device_id=place, device_id_type=MESH)

    @pl.when(has_up)
    def _():
        pl.semaphore_signal(barrier, inc=1, device_id=rad_up, device_id_type=MESH)

    @pl.when(has_dn)
    def _():
        pl.semaphore_signal(barrier, inc=1, device_id=rad_dn, device_id_type=MESH)

    pending = []

    def bring(src, dst):
        copy = pltpu.make_async_copy(src, dst, in_sem.at[len(pending)])
        copy.start()
        pending.append(copy)
        return copy

    states = (as_, fs)
    memories = (am, fm)
    got_stress = [bring(states[s].at[pl.ds(3, 6)], raw.at[s, pl.ds(3, 6)]) for s in (ADJ, FWD)]

    got_small = [
        bring(a, b)
        for a, b in (
            (ze_h, ze), (zr_h, zr), (zw_h, zw), (sc_h, sc_v), (sf_h, sf_v), (rc_h, rc_v),
            (rr_h, rr_v), (zone_h, zone_v), (mu_h, mu_v),
        )
    ]
    got_vel = [bring(states[s].at[pl.ds(0, 3)], raw.at[s, pl.ds(0, 3)]) for s in (ADJ, FWD)]

    lane = lax.broadcasted_iota(jnp.int32, (NAZ, LANES), 1)
    lane8 = lax.broadcasted_iota(jnp.int32, (8, LANES), 1)

    def where_f(cond, value):
        return jnp.where(cond, f32(value), f32(0.0))

    def base(t, r, half):
        return 12 * (2 * r + half) + 4 * t

    ends = (lane8 < 2) | (lane8 >= 126)

    def pack_depth(sys, phase, gets):
        parcel = None
        for r in range(NRAD):
            for t, get in enumerate(gets):
                g = get(r)
                for half in range(2):
                    piece = jnp.where(ends, g[8 * half: 8 * half + 8], 0.0)
                    if base(t, r, half):
                        piece = pltpu.roll(piece, base(t, r, half), 1)
                    parcel = piece if parcel is None else parcel + piece
        msg_out[sys, phase] = parcel

    def local_depth(sys, gets, aheads):
        for t in range(3):
            for r in range(NRAD):
                g = gets[t](r)
                m1 = pltpu.roll(g, LANES - 1, 1)
                r1 = pltpu.roll(g, 1, 1)
                if aheads[t]:
                    m2 = pltpu.roll(g, LANES - 2, 1)
                    dz[sys, t, r] = (where_f(lane < 127, C1) * m1 - C1 * g - where_f(lane < 126, C2) * m2
                                     + where_f(lane >= 1, C2) * r1)
                else:
                    r2 = pltpu.roll(g, 2, 1)
                    dz[sys, t, r] = (C1 * g - where_f(lane >= 1, C1) * r1 - where_f(lane < 127, C2) * m1
                                     + where_f(lane >= 2, C2) * r2)

    slot = lax.rem(lax.rem(lane8 + 2, LANES), 12)
    place_in = lax.rem(slot, 4)
    which = lax.div(slot, 4)

    def wraps(sys, phase, aheads):
        x = msg_in[sys, phase]
        ahead = None
        for t in range(3):
            if aheads[t]:
                ahead = (which == t) if ahead is None else ahead | (which == t)
        behind = jnp.logical_not(ahead)
        m1, m2 = pltpu.roll(x, LANES - 1, 1), pltpu.roll(x, LANES - 2, 1)
        r1, r2 = pltpu.roll(x, 1, 1), pltpu.roll(x, 2, 1)
        at126, at127, at0, at1 = [place_in == i for i in range(4)]
        k_m1 = jnp.where(at127, jnp.where(ahead, f32(C1), f32(-C2)), 0.0)
        k_m2 = where_f(ahead & (at126 | at127), -C2)
        k_r1 = jnp.where(at0, jnp.where(ahead, f32(C2), f32(-C1)), 0.0)
        k_r2 = where_f(behind & (at0 | at1), C2)
        return k_m1 * m1 + k_m2 * m2 + k_r1 * r1 + k_r2 * r2

    mine = lane8 - 126 * (1 - dep)
    edge = (mine >= 0) & (mine < 2)

    def depth_diff(sys, parcel, t, r):
        halves = []
        for half in range(2):
            shift = base(t, r, half)
            piece = pltpu.roll(parcel, LANES - shift, 1) if shift else parcel
            halves.append(jnp.where(edge, piece, 0.0))
        return dz[sys, t, r] + jnp.concatenate(halves, axis=0)

    started = []

    def plan_of(phase):
        return VEL_PLAN if phase % 2 else STRESS_PLAN

    def keep(sys, phase, c, r, value):
        ref = vel if phase % 2 else stress
        ref[sys, phase // 2, c, r, LO:HI] = value
        for way in range(2):
            if (c, r) in plan_of(phase)[way]:
                rad_out[sys, phase, way, plan_of(phase)[way].index((c, r))] = value

    def exchange(sys, phase, field, az_from, gets):
        number = [0]
        legs, up_legs, dn_legs = [], [], []

        def leg(src, dst, place, group):
            n = number[0]
            number[0] += 1

            def make():
                return pltpu.make_async_remote_copy(
                    src_ref=src(), dst_ref=dst(),
                    send_sem=send_sem.at[sys, phase, n], recv_sem=recv_sem.at[sys, phase, n],
                    device_id=place, device_id_type=MESH,
                )

            make().start()
            group.append(make)

        def layers(ref, way):
            return lambda: ref.at[sys, phase, way, pl.ds(0, len(plan_of(phase)[way]))]

        @pl.when(has_up)
        def _():
            leg(layers(rad_out, 0), layers(rad_in, 0), rad_up, up_legs)

        @pl.when(has_dn)
        def _():
            leg(layers(rad_out, 1), layers(rad_in, 1), rad_dn, dn_legs)

        for way, row, place in ((0, HI - 2, az_up), (1, LO, az_dn)):
            for i in range(3):
                for r in range(NRAD):
                    az_out[sys, phase, way, i, 2 * r: 2 * r + 2] = field[az_from + i, r, row: row + 2]
            leg(lambda way=way: az_out.at[sys, phase, way], lambda way=way: az_in.at[sys, phase, way],
                place, legs)
        pack_depth(sys, phase, gets)
        leg(lambda: msg_out.at[sys, phase], lambda: msg_in.at[sys, phase], dep_other, legs)
        groups = legs, up_legs, dn_legs, (sys, phase, field, az_from)
        started.append(groups)
        return groups

    def arrive(groups):
        legs, up_legs, dn_legs, (sys, phase, field, az_from) = groups
        for make in legs:
            make().wait_recv()
        for way, row in ((0, LO - 2), (1, HI)):
            for i in range(3):
                for r in range(NRAD):
                    field[az_from + i, r, row: row + 2] = az_in[sys, phase, way, i, 2 * r: 2 * r + 2]

        @pl.when(has_dn)
        def _():
            for make in up_legs:
                make().wait_recv()

        @pl.when(has_up)
        def _():
            for make in dn_legs:
                make().wait_recv()

    def rows(r):
        return pl.ds(r, NAZ, stride=NRAD)

    def stress_field(sys, step):
        return View(stress, sys, step)

    def vel_field(sys, step):
        return View(vel, sys, step)

    STRESS_AHEAD = (False, False, True)
    VEL_AHEAD = (False, True, True)

    def send_stress(sys, step):
        field = stress_field(sys, step)
        gets = [lambda r, c=c: field[c, r, LO:HI] for c in (RZ, TZ, ZZ)]
        groups = exchange(sys, 2 * step, field, RT, gets)
        local_depth(sys, gets, STRESS_AHEAD)
        return groups

    def send_vel(sys, step):
        field = vel_field(sys, step)
        gets = [lambda r, c=c: field[c, r, LO:HI] for c in (2, 0, 1)]
        groups = exchange(sys, 2 * step + 1, field, 0, gets)
        local_depth(sys, gets, VEL_AHEAD)
        return groups

    def rad4(sys, phase, c, r, first):
        field = vel if phase % 2 else stress
        up, down = plan_of(phase)
        found = []
        for k in range(r + first, r + first + 4):
            if k < 0:
                found.append(rad_in[sys, phase, 0, up.index((c, k + NRAD))])
            elif k >= NRAD:
                found.append(rad_in[sys, phase, 1, down.index((c, k - NRAD))])
            else:
                found.append(field[sys, phase // 2, c, k, LO:HI])
        return found

    def az4(field, c, r, first):
        return [field[c, r, LO + first + i: HI + first + i] for i in range(4)]

    def velocity_update(sys, step):
        field = stress_field(sys, step)
        parcel = wraps(sys, 2 * step, STRESS_AHEAD)
        for r in range(NRAD):
            inv_s, inv_c, inv_sa, inv_ca = [geo[i, r] for i in range(4)]
            if step == 0:
                old = [raw[sys, c, rows(r)] for c in range(3)]
            else:
                old = [vel[sys, 0, c, r, LO:HI] for c in range(3)]
            s_rr, s_tt = field[RR, r, LO:HI], field[TT, r, LO:HI]
            s_rt, s_rz = field[RT, r, LO:HI], field[RZ, r, LO:HI]
            push = [
                forward4(*rad4(sys, 2 * step, RR, r, -1)) + backward4(*az4(field, RT, r, -2)) * inv_sa
                + depth_diff(sys, parcel, 0, r) + (s_rr - s_tt) * inv_s,
                backward4(*rad4(sys, 2 * step, RT, r, -2)) + forward4(*az4(field, TT, r, -1)) * inv_ca
                + depth_diff(sys, parcel, 1, r) + 2.0 * s_rt * inv_c,
                backward4(*rad4(sys, 2 * step, RZ, r, -2)) + backward4(*az4(field, TZ, r, -2)) * inv_ca
                + depth_diff(sys, parcel, 2, r) + s_rz * inv_c,
            ]
            gain = mat[0, r]
            for c in range(3):
                keep(sys, 2 * step + 1, c, r, old[c] + gain * (push[c] + inj[sys, step, c, r]))

    def strain_at(sys, step, parcel, r):
        field = vel_field(sys, step)
        inv_s, inv_c, inv_sa, inv_ca = [geo[i, r] for i in range(4)]
        v_r, v_t = field[0, r, LO:HI], field[1, r, LO:HI]
        return [
            backward4(*rad4(sys, 2 * step + 1, 0, r, -2)),
            backward4(*az4(field, 1, r, -2)) * inv_ca + v_r * inv_c,
            depth_diff(sys, parcel, 0, r),
            0.5 * (forward4(*rad4(sys, 2 * step + 1, 1, r, -1)) + forward4(*az4(field, 0, r, -1)) * inv_sa
                   - v_t * inv_s),
            0.5 * (depth_diff(sys, parcel, 1, r) + forward4(*rad4(sys, 2 * step + 1, 2, r, -1))),
            0.5 * (depth_diff(sys, parcel, 2, r) + forward4(*az4(field, 2, r, -1)) * inv_ca),
        ]

    def load_state(sys):
        got_stress[sys].wait()
        for c in range(6):
            for r in range(NRAD):
                keep(sys, 0, c, r, raw[sys, IN_STATE[c], rows(r)])

    load_state(ADJ)
    pl.semaphore_wait(barrier, 3 + has_up.astype(jnp.int32) + has_dn.astype(jnp.int32))
    legs_s = [None, None]
    legs_v = [None, None]
    legs_s[ADJ] = send_stress(ADJ, 0)
    load_state(FWD)
    legs_s[FWD] = send_stress(FWD, 0)
    got_mem = [bring(memories[s], mem.at[s]) for s in (ADJ, FWD)]

    @pl.when(rad == 0)
    def _():
        rad_in[:, :, 0] = jnp.zeros((2, 4, 5, NAZ, LANES), f32)

    @pl.when(rad == n_rad - 1)
    def _():
        rad_in[:, :, 1] = jnp.zeros((2, 4, 5, NAZ, LANES), f32)

    for copy in got_small:
        copy.wait()
    angle = 2.0 * math.pi / (NAZ * n_az)
    inner = (NAZ * n_az) / (2.0 * math.pi)
    for r in range(NRAD):
        centre = jnp.full((NAZ, LANES), f32(inner), f32) + (rad * NRAD + r).astype(f32)
        staggered = centre + 0.5
        geo[0, r] = 1.0 / staggered
        geo[1, r] = 1.0 / centre
        geo[2, r] = 1.0 / (staggered * angle)
        geo[3, r] = 1.0 / (centre * angle)

    betas = []
    for r in range(NRAD):
        zone = zone_v[rows(r)]
        looked = [jnp.zeros((NAZ, LANES), f32) for _ in range(8)]
        for number in range(8):
            hit = zone == number
            for t in range(8):
                ref, row = (ze, t) if t < 2 else (zr, t - 2) if t < 5 else (zw, t - 5)
                looked[t] = jnp.where(hit, ref[row, number], looked[t])
        lame, buoyancy = looked[0], looked[1]
        alpha = [DT * looked[2 + i] for i in range(3)]
        weight = looked[5:8]
        beta = [1.0 - a for a in alpha]
        share = [a * w for a, w in zip(alpha, weight)]
        gain = DT * (1.0 - (share[0] + share[1] + share[2]))
        later = DT * (beta[0] * share[0] + beta[1] * share[1] + beta[2] * share[2])
        doubled = 2.0 * mu_v[rows(r)]
        mat[0, r] = DT * buoyancy
        mat[1, r] = gain * lame
        mat[2, r] = gain * doubled
        mat[3, r] = later * lame
        mat[4, r] = later * doubled
        for i in range(3):
            mat[5 + i, r] = beta[i]

    def inject(sys, cells_ref, force_ref, count):
        cells = cells_ref[...]
        around = lax.shift_right_logical(cells, 13) - NAZ * az
        radial = (lax.shift_right_logical(cells, 8) & 31) - NRAD * rad
        depth = (cells & 255) - LANES * dep
        inside = (around >= 0) & (around < NAZ) & (radial >= 0) & (radial < NRAD)
        key = jnp.where(inside, radial * NAZ + around, -1)
        here = lax.broadcasted_iota(jnp.int32, (NRAD * NAZ, count), 0) == key
        lanes = (lax.broadcasted_iota(jnp.int32, (LANES, count), 0) == depth).astype(f32)
        for step in range(2):
            for c in range(3):
                picked = jnp.where(here, force_ref[c, step: step + 1, :], 0.0)
                total = lax.dot_general(
                    picked, lanes, (((1,), (1,)), ((), ())),
                    precision=lax.Precision.HIGHEST, preferred_element_type=f32,
                )
                for r in range(NRAD):
                    inj[sys, step, c, r] = total[r * NAZ: (r + 1) * NAZ]

    inject(ADJ, rc_v, rr_v, rc_v.shape[1])
    inject(FWD, sc_v, sf_v, sc_v.shape[1])
    for sys in (ADJ, FWD):
        got_vel[sys].wait()

    def advance_velocity(sys, step):
        arrive(legs_s[sys])
        velocity_update(sys, step)
        legs_v[sys] = send_vel(sys, step)

    for sys in (ADJ, FWD):
        advance_velocity(sys, 0)

    for sys in (ADJ, FWD):
        got_mem[sys].wait()
        for r in range(NRAD):
            beta = [mat[5 + i, r] for i in range(3)]
            for e in range(6):
                m = [beta[i] * mem[sys, 6 * i + e, rows(r)] for i in range(3)]
                a1[sys, e, r] = raw[sys, 3 + e, rows(r)] - DT * (m[0] + m[1] + m[2])
                if sys == ADJ:
                    a2[e, r] = DT * (beta[0] * m[0] + beta[1] * m[1] + beta[2] * m[2])

    def first_stress(sys):
        arrive(legs_v[sys])
        parcel = wraps(sys, 1, VEL_AHEAD)
        for r in range(NRAD):
            e = strain_at(sys, 0, parcel, r)
            dilation = e[0] + e[1] + e[2]
            common = mat[1, r] * dilation
            gm = mat[2, r]
            for i in range(6):
                strain[sys, 0, i, r] = e[i]
                change = gm * e[i] + common if i < 3 else gm * e[i]
                keep(sys, 2, STRAIN_ORDER[i], r, a1[sys, i, r] + change)
        legs_s[sys] = send_stress(sys, 1)

    for sys in (ADJ, FWD):
        first_stress(sys)

    for r in range(NRAD):
        e = [strain[ADJ, 0, i, r] for i in range(6)]
        common = mat[3, r] * (e[0] + e[1] + e[2])
        hm = mat[4, r]
        for i in range(6):
            drop = hm * e[i] + common if i < 3 else hm * e[i]
            a2[i, r] = stress[ADJ, 1, STRAIN_ORDER[i], r, LO:HI] - a2[i, r] - drop

    for sys in (ADJ, FWD):
        advance_velocity(sys, 1)
    for r in range(NRAD):
        for c in range(3):
            out_v[c, rows(r)] = vel[ADJ, 1, c, r, LO:HI]

    def product(e, f):
        return 2.0 * DT * (e[0] * f[0] + e[1] * f[1] + e[2] * f[2]
                           + 2.0 * (e[3] * f[3] + e[4] * f[4] + e[5] * f[5]))

    arrive(legs_v[ADJ])
    parcel = wraps(ADJ, 3, VEL_AHEAD)
    for r in range(NRAD):
        e = strain_at(ADJ, 1, parcel, r)
        common = mat[1, r] * (e[0] + e[1] + e[2])
        gm = mat[2, r]
        for i in range(6):
            change = gm * e[i] + common if i < 3 else gm * e[i]
            out_v[3 + i, rows(r)] = a2[i, r] + change
        a1[ADJ, 0, r] = product(e, [strain[FWD, 0, i, r] for i in range(6)])

    arrive(legs_v[FWD])
    parcel = wraps(FWD, 3, VEL_AHEAD)
    for r in range(NRAD):
        e = strain_at(FWD, 1, parcel, r)
        grad_v[rows(r)] = a1[ADJ, 0, r] + product(e, [strain[ADJ, 0, i, r] for i in range(6)])

    for legs, _, _, _ in started:
        for make in legs:
            make().wait_send()

    @pl.when(has_up)
    def _():
        for _, up_legs, _, _ in started:
            for make in up_legs:
                make().wait_send()

    @pl.when(has_dn)
    def _():
        for _, _, dn_legs, _ in started:
            for make in dn_legs:
                make().wait_send()


def hand_on(grad_in, adj_in, grad_out, adj_out, sems):
    copies = [pltpu.make_async_copy(adj_in, adj_out, sems.at[0]),
              pltpu.make_async_copy(grad_in, grad_out, sems.at[1])]
    for copy in copies:
        copy.start()
    for copy in copies:
        copy.wait()


def shards(
    forward_state, forward_memory, adjoint_state, adjoint_memory, shear_modulus, zone,
    zone_elastic, zone_rates, zone_weights, source_cells, source_force, receiver_cells,
    receiver_residual,
):
    cells = NAZ * NRAD
    nsrc, nrec = source_cells.shape[0], receiver_cells.shape[0]
    block = (NRAD, NAZ, LANES)
    vmem = pltpu.VMEM
    hbm = pl.BlockSpec(memory_space=pltpu.HBM)
    gradient, adjoint_out = pl.pallas_call(
        kernel,
        out_shape=(vmem((cells, LANES), f32), vmem((9, cells, LANES), f32)),
        in_specs=[hbm] * 13,
        out_specs=(pl.BlockSpec(memory_space=pltpu.VMEM),) * 2,
        scratch_shapes=[
            vmem((2, 9, cells, LANES), f32),
            vmem((2, 18, cells, LANES), f32),
            vmem((cells, LANES), f32),
            vmem((cells, LANES), jnp.int32),
            pltpu.SMEM((2, 8), f32),
            pltpu.SMEM((3, 8), f32),
            pltpu.SMEM((3, 8), f32),
            vmem((1, nsrc), jnp.int32),
            vmem((3, 2, nsrc), f32),
            vmem((1, nrec), jnp.int32),
            vmem((3, 2, nrec), f32),
            vmem((2, 2, 6, NRAD, NAZ + 16, LANES), f32),
            vmem((2, 2, 3, NRAD, NAZ + 16, LANES), f32),
            vmem((2, 3) + block, f32),
            vmem((2, 4, 2, 5, NAZ, LANES), f32),
            vmem((2, 4, 2, 5, NAZ, LANES), f32),
            vmem((2, 4, 2, 3, 8, LANES), f32),
            vmem((2, 4, 2, 3, 8, LANES), f32),
            vmem((2, 4, 8, LANES), f32),
            vmem((2, 4, 8, LANES), f32),
            vmem((2, 1, 6) + block, f32),
            vmem((2, 6) + block, f32),
            vmem((6,) + block, f32),
            vmem((2, 2, 3) + block, f32),
            vmem((4,) + block, f32),
            vmem((8,) + block, f32),
            pltpu.SemaphoreType.DMA((16,)),
            pltpu.SemaphoreType.DMA((2, 4, 5)),
            pltpu.SemaphoreType.DMA((2, 4, 5)),
        ],
        compiler_params=pltpu.CompilerParams(
            collective_id=0, has_side_effects=True, vmem_limit_bytes=60 * 2**20
        ),
        name="window",
    )(
        forward_state.reshape(9, cells, LANES),
        forward_memory.reshape(18, cells, LANES),
        adjoint_state.reshape(9, cells, LANES),
        adjoint_memory.reshape(18, cells, LANES),
        shear_modulus.reshape(cells, LANES),
        zone.reshape(cells, LANES),
        zone_elastic, zone_rates, zone_weights,
        source_cells.reshape(1, nsrc), source_force.transpose(1, 0, 2),
        receiver_cells.reshape(1, nrec), receiver_residual.transpose(1, 0, 2),
    )
    gradient, adjoint_out = pl.pallas_call(
        hand_on,
        out_shape=(
            jax.ShapeDtypeStruct((cells, LANES), f32),
            jax.ShapeDtypeStruct((9, cells, LANES), f32),
        ),
        in_specs=[pl.BlockSpec(memory_space=pl.ANY)] * 2,
        out_specs=(hbm, hbm),
        scratch_shapes=[pltpu.SemaphoreType.DMA((2,))],
        compiler_params=pltpu.CompilerParams(vmem_limit_bytes=2**20),
        name="hand_on",
    )(gradient, adjoint_out)
    return gradient.reshape(NAZ, NRAD, LANES), adjoint_out.reshape(9, NAZ, NRAD, LANES)


def solution(mesh):
    return jax.shard_map(
        shards,
        mesh=mesh,
        in_specs=(
            P(None, "az", "rad", "dep"),
            P(None, None, "az", "rad", "dep"),
            P(None, "az", "rad", "dep"),
            P(None, None, "az", "rad", "dep"),
            P("az", "rad", "dep"),
            P("az", "rad", "dep"),
            P(), P(), P(), P(), P(), P(), P(),
        ),
        out_specs=(P("az", "rad", "dep"), P(None, "az", "rad", "dep")),
        check_vma=False,
    )
```

```python
import math

import jax
import jax.numpy as jnp
from jax import lax
from jax.experimental import pallas as pl
from jax.experimental.pallas import tpu as pltpu
from jax.sharding import PartitionSpec as P

MESH = pl.DeviceIdType.MESH
f32 = jnp.float32

DT = 0.2
C1 = 1.125
C2 = 1.0 / 24.0

RR, RZ, RT, TT, TZ, ZZ = range(6)
IN_STATE = {RR: 3, TT: 4, ZZ: 5, RT: 6, RZ: 7, TZ: 8}
STRAIN_ORDER = (RR, TT, ZZ, RT, RZ, TZ)

ADJ, FWD = 0, 1
NAZ, NRAD, LANES = 16, 4, 128
LO, HI = 8, 8 + NAZ
STRESS_PLAN = (((RR, 3), (RZ, 2), (RZ, 3), (RT, 2), (RT, 3)), ((RR, 0), (RR, 1), (RZ, 0), (RT, 0)))
VEL_PLAN = (((0, 2), (0, 3), (1, 3), (2, 3)), ((0, 0), (1, 0), (1, 1), (2, 0), (2, 1)))


STRESS_AHEAD, VEL_AHEAD = (False, False, True), (False, True, True)
STRESS_AZ_AHEAD, VEL_AZ_AHEAD = (False, True, False), (True, False, True)


class View:
    def __init__(self, ref, sys, step):
        self.ref, self.lead = ref, (sys, step)

    def __getitem__(self, index):
        return self.ref[self.lead + index]

    def __setitem__(self, index, value):
        self.ref[self.lead + index] = value


def forward4(before, here, after, after2):
    return C1 * (after - here) - C2 * (after2 - before)


def backward4(before2, before, here, after):
    return C1 * (here - before) - C2 * (after - before2)


def kernel(
    fs, fm, as_, am, mu_h, zone_h, ze_h, zr_h, zw_h, sc_h, sf_h, rc_h, rr_h,
    grad_v, out_v,
    raw, mem, mu_v, zone_v, ze, zr, zw, sc_v, sf_v, rc_v, rr_v,
    stress, vel, acc, azc, rad_out, rad_in, crit_out, crit_in, gain_in, beside, az_out, az_in, msg_out, msg_in, strain, a1, a2, inj, geo, mat,
    in_sem, send_sem, recv_sem, gain_sem,
):
    n_az, n_rad, n_dep = lax.axis_size("az"), lax.axis_size("rad"), lax.axis_size("dep")
    az, rad, dep = lax.axis_index("az"), lax.axis_index("rad"), lax.axis_index("dep")
    az_up, az_dn = {"az": lax.rem(az + 1, n_az)}, {"az": lax.rem(az + n_az - 1, n_az)}
    rad_up, rad_dn = {"rad": rad + 1}, {"rad": rad - 1}
    dep_other = {"dep": 1 - dep}

    has_dn, has_up = rad > 0, rad < n_rad - 1
    barrier = pltpu.get_barrier_semaphore()
    for place in (az_up, az_dn, dep_other):
        pl.semaphore_signal(barrier, inc=1, device_id=place, device_id_type=MESH)

    @pl.when(has_up)
    def _():
        pl.semaphore_signal(barrier, inc=1, device_id=rad_up, device_id_type=MESH)

    @pl.when(has_dn)
    def _():
        pl.semaphore_signal(barrier, inc=1, device_id=rad_dn, device_id_type=MESH)

    pending = []

    def bring(src, dst):
        copy = pltpu.make_async_copy(src, dst, in_sem.at[len(pending)])
        copy.start()
        pending.append(copy)
        return copy

    states = (as_, fs)
    memories = (am, fm)
    got_stress = [bring(states[s].at[pl.ds(3, 6)], raw.at[s, pl.ds(3, 6)]) for s in (ADJ, FWD)]

    lane = lax.broadcasted_iota(jnp.int32, (NAZ, LANES), 1)
    lane8 = lax.broadcasted_iota(jnp.int32, (8, LANES), 1)

    def where_f(cond, value):
        return jnp.where(cond, f32(value), f32(0.0))

    def base(t, r, half):
        return 12 * (2 * r + half) + 4 * t

    ends = (lane8 < 2) | (lane8 >= 126)

    def pack_depth(sys, phase, gets):
        parcel = None
        for r in range(NRAD):
            for t, get in enumerate(gets):
                g = get(r)
                for half in range(2):
                    piece = jnp.where(ends, g[8 * half: 8 * half + 8], 0.0)
                    if base(t, r, half):
                        piece = pltpu.roll(piece, base(t, r, half), 1)
                    parcel = piece if parcel is None else parcel + piece
        msg_out[sys, phase] = parcel

    def depth_local(g, ahead):
        m1 = pltpu.roll(g, LANES - 1, 1)
        r1 = pltpu.roll(g, 1, 1)
        if ahead:
            m2 = pltpu.roll(g, LANES - 2, 1)
            return (where_f(lane < 127, C1) * m1 - C1 * g - where_f(lane < 126, C2) * m2
                    + where_f(lane >= 1, C2) * r1)
        r2 = pltpu.roll(g, 2, 1)
        return (C1 * g - where_f(lane >= 1, C1) * r1 - where_f(lane < 127, C2) * m1
                + where_f(lane >= 2, C2) * r2)

    slot = lax.rem(lax.rem(lane8 + 2, LANES), 12)
    place_in = lax.rem(slot, 4)
    which = lax.div(slot, 4)

    def wraps(sys, phase, aheads):
        x = msg_in[sys, phase]
        ahead = None
        for t in range(3):
            if aheads[t]:
                ahead = (which == t) if ahead is None else ahead | (which == t)
        behind = jnp.logical_not(ahead)
        m1, m2 = pltpu.roll(x, LANES - 1, 1), pltpu.roll(x, LANES - 2, 1)
        r1, r2 = pltpu.roll(x, 1, 1), pltpu.roll(x, 2, 1)
        at126, at127, at0, at1 = [place_in == i for i in range(4)]
        k_m1 = jnp.where(at127, jnp.where(ahead, f32(C1), f32(-C2)), 0.0)
        k_m2 = where_f(ahead & (at126 | at127), -C2)
        k_r1 = jnp.where(at0, jnp.where(ahead, f32(C2), f32(-C1)), 0.0)
        k_r2 = where_f(behind & (at0 | at1), C2)
        return k_m1 * m1 + k_m2 * m2 + k_r1 * r1 + k_r2 * r2

    mine = lane8 - 126 * (1 - dep)
    edge = (mine >= 0) & (mine < 2)

    def depth_halo(parcel, t, r):
        halves = []
        for half in range(2):
            shift = base(t, r, half)
            piece = pltpu.roll(parcel, LANES - shift, 1) if shift else parcel
            halves.append(jnp.where(edge, piece, 0.0))
        return jnp.concatenate(halves, axis=0)

    started = []

    def plan_of(phase):
        return VEL_PLAN if phase % 2 else STRESS_PLAN

    def keep(sys, phase, c, r, value):
        ref = vel if phase % 2 else stress
        ref[sys, phase // 2, c, r, LO:HI] = value
        if phase % 2:
            return
        for way in range(2):
            if (c, r) in plan_of(phase)[way]:
                rad_out[sys, phase, way, plan_of(phase)[way].index((c, r))] = value

    def exchange(sys, phase, field, az_from, gets):
        number = [0]
        legs, up_legs, dn_legs = [], [], []

        def leg(src, dst, place, group):
            n = number[0]
            number[0] += 1

            def make():
                return pltpu.make_async_remote_copy(
                    src_ref=src(), dst_ref=dst(),
                    send_sem=send_sem.at[sys, phase, n], recv_sem=recv_sem.at[sys, phase, n],
                    device_id=place, device_id_type=MESH,
                )

            make().start()
            group.append(make)

        def radial(way, out):
            if phase % 2:
                return (crit_out if out else crit_in).at[sys, phase // 2, way]
            return (rad_out if out else rad_in).at[sys, phase, way, pl.ds(0, len(plan_of(phase)[way]))]

        @pl.when(has_up)
        def _():
            leg(lambda: radial(0, True), lambda: radial(0, False), rad_up, up_legs)

        @pl.when(has_dn)
        def _():
            leg(lambda: radial(1, True), lambda: radial(1, False), rad_dn, dn_legs)

        yield None
        for way, row, place in ((0, HI - 2, az_up), (1, LO, az_dn)):
            for i in range(3):
                for r in range(NRAD):
                    az_out[sys, phase, way, i, 2 * r: 2 * r + 2] = field[az_from + i, r, row: row + 2]
            leg(lambda way=way: az_out.at[sys, phase, way], lambda way=way: az_in.at[sys, phase, way],
                place, legs)
        pack_depth(sys, phase, gets)
        leg(lambda: msg_out.at[sys, phase], lambda: msg_in.at[sys, phase], dep_other, legs)
        groups = legs, up_legs, dn_legs, (sys, phase)
        started.append(groups)
        yield groups

    def radial_pair(make):
        @pl.when(has_up)
        def _():
            make(0).start()

        @pl.when(has_dn)
        def _():
            make(1).start()

        started.append(([], [lambda: make(0)], [lambda: make(1)], (None, 0)))
        return make

    def landed(make):
        @pl.when(has_dn)
        def _():
            make(0).wait_recv()

        @pl.when(has_up)
        def _():
            make(1).wait_recv()

    def send_gain():
        return radial_pair(lambda way: pltpu.make_async_remote_copy(
            src_ref=mat.at[0, pl.ds(2 * (1 - way), 2)], dst_ref=gain_in.at[way],
            send_sem=gain_sem.at[0, way], recv_sem=gain_sem.at[1, way],
            device_id=(rad_up, rad_dn)[way], device_id_type=MESH,
        ))

    def send_ahead(sys, step):
        phase = 2 * step + 1
        for way in range(2):
            for i, (c, r) in enumerate(VEL_PLAN[way]):
                rad_out[sys, phase, way, i] = acc[sys, c, r]

        def make(way):
            count = pl.ds(0, len(VEL_PLAN[way]))
            return pltpu.make_async_remote_copy(
                src_ref=rad_out.at[sys, phase, way, count], dst_ref=rad_in.at[sys, phase, way, count],
                send_sem=send_sem.at[sys, phase, 5 + way], recv_sem=recv_sem.at[sys, phase, 5 + way],
                device_id=(rad_up, rad_dn)[way], device_id_type=MESH,
            )

        return radial_pair(make)

    PUSHED_BY = ((RR, True), (RT, False), (RZ, False))

    def rebuild(sys, step, ahead_copies):
        landed(ahead_copies)
        phase = 2 * step + 1
        for way in range(2):
            for i, (c, r) in enumerate(VEL_PLAN[way]):
                comp, ahead = PUSHED_BY[c]
                first = -1 if ahead else -2
                total = None
                for shift, factor in enumerate((C2, -C1, C1, -C2)):
                    k = r + first + shift
                    if 0 <= k < NRAD:
                        continue
                    term = factor * stress[sys, step, comp, k % NRAD, LO:HI]
                    total = term if total is None else total + term
                rad_in[sys, phase, way, i] = rad_in[sys, phase, way, i] + gain_in[way, r % 2] * total

    def add_late(sys, step):
        phase = 2 * step + 1
        for way in range(2):
            lanes_tile = crit_in[sys, step, way, 3]
            for i, (c, r) in enumerate(VEL_PLAN[way]):
                rad_in[sys, phase, way, i] = (rad_in[sys, phase, way, i]
                                              + gain_in[way, r % 2] * depth_halo(lanes_tile, c, r))
                for side, row in ((0, 0), (1, NAZ - 2)):
                    source = 4 * side + 2 * (r % 2)
                    rad_in[sys, phase, way, i, row: row + 2] = (
                        rad_in[sys, phase, way, i, row: row + 2]
                        + beside[way, 0 if c == 0 else 1, r % 2, row: row + 2]
                        * crit_in[sys, step, way, c, source: source + 2])

    even = lax.rem(lax.broadcasted_iota(jnp.int32, (8, LANES), 0), 2) == 0

    def arrive(groups):
        legs, up_legs, dn_legs, (sys, phase) = groups
        for make in legs:
            make().wait_recv()
        for i, ahead in enumerate(VEL_AZ_AHEAD if phase % 2 else STRESS_AZ_AHEAD):
            low, high = az_in[sys, phase, 0, i], az_in[sys, phase, 1, i]
            if ahead:
                low = jnp.where(even, C2 * pltpu.roll(low, 7, 0), 0.0)
                high = jnp.where(even, 0.0, C1 * pltpu.roll(high, 1, 0)) - C2 * high
            else:
                low = C2 * low - jnp.where(even, C1 * pltpu.roll(low, 7, 0), 0.0)
                high = jnp.where(even, 0.0, -C2 * pltpu.roll(high, 1, 0))
            az_in[sys, phase, 0, i] = low
            az_in[sys, phase, 1, i] = high
            for r in range(NRAD):
                azc[sys, i, r, 0:2] = az_in[sys, phase, 0, i, 2 * r: 2 * r + 2]
                azc[sys, i, r, NAZ - 2: NAZ] = az_in[sys, phase, 1, i, 2 * r: 2 * r + 2]

        @pl.when(has_dn)
        def _():
            for make in up_legs:
                make().wait_recv()

        @pl.when(has_up)
        def _():
            for make in dn_legs:
                make().wait_recv()

        if phase % 2:
            add_late(sys, phase // 2)

    def rows(r):
        return pl.ds(r, NAZ, stride=NRAD)

    def stress_field(sys, step):
        return View(stress, sys, step)

    def vel_field(sys, step):
        return View(vel, sys, step)

    def stress_gets(sys, step):
        field = stress_field(sys, step)
        return [lambda r, c=c: field[c, r, LO:HI] for c in (RZ, TZ, ZZ)]

    def vel_gets(sys, step):
        field = vel_field(sys, step)
        return [lambda r, c=c: field[c, r, LO:HI] for c in (2, 0, 1)]

    def send_stress(sys, step):
        steps = exchange(sys, 2 * step, stress_field(sys, step), RT, stress_gets(sys, step))
        next(steps)
        return next(steps)

    def start_vel(sys, step):
        return exchange(sys, 2 * step + 1, vel_field(sys, step), 0, vel_gets(sys, step))

    def rad_local(sys, phase, c, r, ahead):
        field = vel if phase % 2 else stress

        def own(k):
            return field[sys, phase // 2, c, k, LO:HI]

        first = -1 if ahead else -2
        factors = {first: C2, first + 1: -C1, first + 2: C1, first + 3: -C2}
        total = None
        for shift, factor in factors.items():
            if 0 <= r + shift < NRAD:
                term = factor * own(r + shift)
                total = term if total is None else total + term
        return total

    def rad_halo(sys, phase, c, r, ahead):
        up, down = plan_of(phase)
        first = -1 if ahead else -2
        factors = {first: C2, first + 1: -C1, first + 2: C1, first + 3: -C2}
        total = None
        for shift, factor in factors.items():
            k = r + shift
            if 0 <= k < NRAD:
                continue
            way, row = (0, up.index((c, k + NRAD))) if k < 0 else (1, down.index((c, k - NRAD)))
            term = factor * rad_in[sys, phase, way, row]
            total = term if total is None else total + term
        return total

    def plus(*terms):
        terms = [t for t in terms if t is not None]
        total = terms[0]
        for t in terms[1:]:
            total = total + t
        return total

    def az4(field, c, r, first):
        return [field[c, r, LO + first + i: HI + first + i] for i in range(4)]

    def velocity_local(sys, step):
        field, phase = stress_field(sys, step), 2 * step
        gets = stress_gets(sys, step)
        for r in range(NRAD):
            inv_s, inv_c, inv_sa, inv_ca = [geo[i, r] for i in range(4)]
            if step == 0:
                old = [raw[sys, c, rows(r)] for c in range(3)]
            else:
                old = [vel[sys, 0, c, r, LO:HI] for c in range(3)]
            s_rr, s_tt = field[RR, r, LO:HI], field[TT, r, LO:HI]
            s_rt, s_rz = field[RT, r, LO:HI], field[RZ, r, LO:HI]
            push = [
                rad_local(sys, phase, RR, r, True) + backward4(*az4(field, RT, r, -2)) * inv_sa
                + depth_local(gets[0](r), False) + (s_rr - s_tt) * inv_s,
                rad_local(sys, phase, RT, r, False) + forward4(*az4(field, TT, r, -1)) * inv_ca
                + depth_local(gets[1](r), False) + 2.0 * s_rt * inv_c,
                rad_local(sys, phase, RZ, r, False) + backward4(*az4(field, TZ, r, -2)) * inv_ca
                + depth_local(gets[2](r), True) + s_rz * inv_c,
            ]
            gain = mat[0, r]
            for c in range(3):
                acc[sys, c, r] = old[c] + gain * (push[c] + inj[sys, step, c, r])

    def velocity_finish(sys, step):
        phase = 2 * step
        parcel = wraps(sys, phase, STRESS_AHEAD)
        for way in range(2):
            start = 4 * (1 - way)
            for c in range(3):
                for side in range(2):
                    crit_out[sys, step, way, c, 4 * side: 4 * side + 4] = (
                        az_in[sys, phase, side, c, start: start + 4])
            crit_out[sys, step, way, 3] = parcel
        steps = start_vel(sys, step)
        next(steps)
        for r in range(NRAD):
            gain = mat[0, r]
            inv = (geo[2, r], geo[3, r], geo[3, r])
            for c, (s, ahead) in enumerate(PUSHED_BY):
                halo = plus(azc[sys, c, r] * inv[c], depth_halo(parcel, c, r),
                            rad_halo(sys, phase, s, r, ahead))
                keep(sys, phase + 1, c, r, acc[sys, c, r] + gain * halo)
        return next(steps)

    def strain_local(sys, step):
        field, phase = vel_field(sys, step), 2 * step + 1
        gets = vel_gets(sys, step)
        for r in range(NRAD):
            inv_s, inv_c, inv_sa, inv_ca = [geo[i, r] for i in range(4)]
            v_r, v_t = field[0, r, LO:HI], field[1, r, LO:HI]
            acc[sys, 0, r] = rad_local(sys, phase, 0, r, False)
            acc[sys, 1, r] = backward4(*az4(field, 1, r, -2)) * inv_ca + v_r * inv_c
            acc[sys, 2, r] = depth_local(gets[0](r), False)
            acc[sys, 3, r] = 0.5 * (rad_local(sys, phase, 1, r, True)
                                    + forward4(*az4(field, 0, r, -1)) * inv_sa - v_t * inv_s)
            acc[sys, 4, r] = 0.5 * (depth_local(gets[1](r), True) + rad_local(sys, phase, 2, r, True))
            acc[sys, 5, r] = 0.5 * (depth_local(gets[2](r), True)
                                    + forward4(*az4(field, 2, r, -1)) * inv_ca)

    def strain_at(sys, step, parcel, r):
        phase = 2 * step + 1
        inv_sa, inv_ca = geo[2, r], geo[3, r]
        halo = [
            rad_halo(sys, phase, 0, r, False),
            azc[sys, 1, r] * inv_ca,
            depth_halo(parcel, 0, r),
            0.5 * plus(azc[sys, 0, r] * inv_sa, rad_halo(sys, phase, 1, r, True)),
            0.5 * plus(depth_halo(parcel, 1, r), rad_halo(sys, phase, 2, r, True)),
            0.5 * (depth_halo(parcel, 2, r) + azc[sys, 2, r] * inv_ca),
        ]
        return [plus(acc[sys, i, r], halo[i]) for i in range(6)]

    def load_state(sys):
        got_stress[sys].wait()
        for c in range(6):
            for r in range(NRAD):
                keep(sys, 0, c, r, raw[sys, IN_STATE[c], rows(r)])

    load_state(ADJ)
    pl.semaphore_wait(barrier, 3 + has_up.astype(jnp.int32) + has_dn.astype(jnp.int32))
    legs_s = [None, None]
    legs_v = [None, None]
    ahead = [None, None]
    legs_s[ADJ] = send_stress(ADJ, 0)
    load_state(FWD)
    legs_s[FWD] = send_stress(FWD, 0)
    got_small = [
        bring(a, b)
        for a, b in (
            (ze_h, ze), (zr_h, zr), (zw_h, zw), (sc_h, sc_v), (sf_h, sf_v), (rc_h, rc_v),
            (rr_h, rr_v), (zone_h, zone_v), (mu_h, mu_v),
        )
    ]
    got_vel = [bring(states[s].at[pl.ds(0, 3)], raw.at[s, pl.ds(0, 3)]) for s in (ADJ, FWD)]
    got_mem = [bring(memories[s], mem.at[s]) for s in (ADJ, FWD)]

    @pl.when(rad == 0)
    def _():
        rad_in[:, :, 0] = jnp.zeros((2, 4, 5, NAZ, LANES), f32)
        crit_in[:, :, 0] = jnp.zeros((2, 2, 4, 8, LANES), f32)
        gain_in[0] = jnp.zeros((2, NAZ, LANES), f32)

    @pl.when(rad == n_rad - 1)
    def _():
        rad_in[:, :, 1] = jnp.zeros((2, 4, 5, NAZ, LANES), f32)
        crit_in[:, :, 1] = jnp.zeros((2, 2, 4, 8, LANES), f32)
        gain_in[1] = jnp.zeros((2, NAZ, LANES), f32)

    for copy in got_small:
        copy.wait()
    angle = 2.0 * math.pi / (NAZ * n_az)
    inner = (NAZ * n_az) / (2.0 * math.pi)
    for r in range(NRAD):
        centre = jnp.full((NAZ, LANES), f32(inner), f32) + (rad * NRAD + r).astype(f32)
        staggered = centre + 0.5
        geo[0, r] = 1.0 / staggered
        geo[1, r] = 1.0 / centre
        geo[2, r] = 1.0 / (staggered * angle)
        geo[3, r] = 1.0 / (centre * angle)

    betas = []
    for r in range(NRAD):
        zone = zone_v[rows(r)]
        looked = [jnp.zeros((NAZ, LANES), f32) for _ in range(8)]
        for number in range(8):
            hit = zone == number
            for t in range(8):
                ref, row = (ze, t) if t < 2 else (zr, t - 2) if t < 5 else (zw, t - 5)
                looked[t] = jnp.where(hit, ref[row, number], looked[t])
        lame, buoyancy = looked[0], looked[1]
        alpha = [DT * looked[2 + i] for i in range(3)]
        weight = looked[5:8]
        beta = [1.0 - a for a in alpha]
        share = [a * w for a, w in zip(alpha, weight)]
        gain = DT * (1.0 - (share[0] + share[1] + share[2]))
        later = DT * (beta[0] * share[0] + beta[1] * share[1] + beta[2] * share[2])
        doubled = 2.0 * mu_v[rows(r)]
        mat[0, r] = DT * buoyancy
        mat[1, r] = gain * lame
        mat[2, r] = gain * doubled
        mat[3, r] = later * lame
        mat[4, r] = later * doubled
        for i in range(3):
            mat[5 + i, r] = beta[i]

    gains = send_gain()

    def inject(sys, cells_ref, force_ref, count):
        cells = cells_ref[...]
        around = lax.shift_right_logical(cells, 13) - NAZ * az
        radial = (lax.shift_right_logical(cells, 8) & 31) - NRAD * rad
        depth = (cells & 255) - LANES * dep
        inside = (around >= 0) & (around < NAZ) & (radial >= 0) & (radial < NRAD)
        key = jnp.where(inside, radial * NAZ + around, -1)
        here = lax.broadcasted_iota(jnp.int32, (NRAD * NAZ, count), 0) == key
        lanes = (lax.broadcasted_iota(jnp.int32, (LANES, count), 0) == depth).astype(f32)
        for step in range(2):
            for c in range(3):
                picked = jnp.where(here, force_ref[c, step: step + 1, :], 0.0)
                total = lax.dot_general(
                    picked, lanes, (((1,), (1,)), ((), ())),
                    precision=lax.Precision.HIGHEST, preferred_element_type=f32,
                )
                for r in range(NRAD):
                    inj[sys, step, c, r] = total[r * NAZ: (r + 1) * NAZ]

    inject(ADJ, rc_v, rr_v, rc_v.shape[1])
    inject(FWD, sc_v, sf_v, sc_v.shape[1])
    for sys in (ADJ, FWD):
        got_vel[sys].wait()
        azc[sys] = jnp.zeros((3, NRAD, NAZ, LANES), f32)
        for step in range(2):
            for row in (0, HI):
                stress[sys, step, RT: RT + 3, :, row: row + 8] = jnp.zeros((3, NRAD, 8, LANES), f32)
                vel[sys, step, :, :, row: row + 8] = jnp.zeros((3, NRAD, 8, LANES), f32)
        velocity_local(sys, 0)
        ahead[sys] = send_ahead(sys, 0)

    def advance_velocity(sys, step):
        arrive(legs_s[sys])
        legs_v[sys] = velocity_finish(sys, step)

    for sys in (ADJ, FWD):
        advance_velocity(sys, 0)
    landed(gains)
    for way in range(2):
        for r in range(2):
            layer = (rad * NRAD + (r - 2 if way == 0 else NRAD + r)).astype(f32)
            centre = jnp.full((NAZ, LANES), f32(inner), f32) + layer
            beside[way, 0, r] = gain_in[way, r] / ((centre + 0.5) * angle)
            beside[way, 1, r] = gain_in[way, r] / (centre * angle)
    for sys in (ADJ, FWD):
        rebuild(sys, 0, ahead[sys])
        strain_local(sys, 0)

    for sys in (ADJ, FWD):
        got_mem[sys].wait()
        for r in range(NRAD):
            beta = [mat[5 + i, r] for i in range(3)]
            for e in range(6):
                m = [beta[i] * mem[sys, 6 * i + e, rows(r)] for i in range(3)]
                a1[sys, e, r] = raw[sys, 3 + e, rows(r)] - DT * (m[0] + m[1] + m[2])
                if sys == ADJ:
                    a2[e, r] = DT * (beta[0] * m[0] + beta[1] * m[1] + beta[2] * m[2])

    def first_stress(sys):
        arrive(legs_v[sys])
        parcel = wraps(sys, 1, VEL_AHEAD)
        for r in range(NRAD):
            e = strain_at(sys, 0, parcel, r)
            dilation = e[0] + e[1] + e[2]
            common = mat[1, r] * dilation
            gm = mat[2, r]
            for i in range(6):
                strain[sys, 0, i, r] = e[i]
                change = gm * e[i] + common if i < 3 else gm * e[i]
                keep(sys, 2, STRAIN_ORDER[i], r, a1[sys, i, r] + change)
        legs_s[sys] = send_stress(sys, 1)

    for sys in (ADJ, FWD):
        first_stress(sys)
    for sys in (ADJ, FWD):
        velocity_local(sys, 1)
        ahead[sys] = send_ahead(sys, 1)

    for r in range(NRAD):
        e = [strain[ADJ, 0, i, r] for i in range(6)]
        common = mat[3, r] * (e[0] + e[1] + e[2])
        hm = mat[4, r]
        for i in range(6):
            drop = hm * e[i] + common if i < 3 else hm * e[i]
            a2[i, r] = stress[ADJ, 1, STRAIN_ORDER[i], r, LO:HI] - a2[i, r] - drop

    for sys in (ADJ, FWD):
        advance_velocity(sys, 1)
    for sys in (ADJ, FWD):
        rebuild(sys, 1, ahead[sys])
        strain_local(sys, 1)
    for r in range(NRAD):
        for c in range(3):
            out_v[c, rows(r)] = vel[ADJ, 1, c, r, LO:HI]

    def product(e, f):
        return 2.0 * DT * (e[0] * f[0] + e[1] * f[1] + e[2] * f[2]
                           + 2.0 * (e[3] * f[3] + e[4] * f[4] + e[5] * f[5]))

    def sent(batch):
        for legs, _, _, _ in batch:
            for make in legs:
                make().wait_send()

        @pl.when(has_up)
        def _():
            for _, up_legs, _, _ in batch:
                for make in up_legs:
                    make().wait_send()

        @pl.when(has_dn)
        def _():
            for _, _, dn_legs, _ in batch:
                for make in dn_legs:
                    make().wait_send()

    sent([g for g in started if g[3][1] != 3])
    arrive(legs_v[ADJ])
    parcel = wraps(ADJ, 3, VEL_AHEAD)
    for r in range(NRAD):
        e = strain_at(ADJ, 1, parcel, r)
        common = mat[1, r] * (e[0] + e[1] + e[2])
        gm = mat[2, r]
        for i in range(6):
            change = gm * e[i] + common if i < 3 else gm * e[i]
            out_v[3 + i, rows(r)] = a2[i, r] + change
        a1[ADJ, 0, r] = product(e, [strain[FWD, 0, i, r] for i in range(6)])

    arrive(legs_v[FWD])
    parcel = wraps(FWD, 3, VEL_AHEAD)
    for r in range(NRAD):
        e = strain_at(FWD, 1, parcel, r)
        grad_v[rows(r)] = a1[ADJ, 0, r] + product(e, [strain[ADJ, 0, i, r] for i in range(6)])

    sent([g for g in started if g[3][1] == 3])


def hand_on(grad_in, adj_in, grad_out, adj_out, sems):
    copies = [pltpu.make_async_copy(adj_in, adj_out, sems.at[0]),
              pltpu.make_async_copy(grad_in, grad_out, sems.at[1])]
    for copy in copies:
        copy.start()
    for copy in copies:
        copy.wait()


def shards(
    forward_state, forward_memory, adjoint_state, adjoint_memory, shear_modulus, zone,
    zone_elastic, zone_rates, zone_weights, source_cells, source_force, receiver_cells,
    receiver_residual,
):
    cells = NAZ * NRAD
    nsrc, nrec = source_cells.shape[0], receiver_cells.shape[0]
    block = (NRAD, NAZ, LANES)
    vmem = pltpu.VMEM
    hbm = pl.BlockSpec(memory_space=pltpu.HBM)
    gradient, adjoint_out = pl.pallas_call(
        kernel,
        out_shape=(vmem((cells, LANES), f32), vmem((9, cells, LANES), f32)),
        in_specs=[hbm] * 13,
        out_specs=(pl.BlockSpec(memory_space=pltpu.VMEM),) * 2,
        scratch_shapes=[
            vmem((2, 9, cells, LANES), f32),
            vmem((2, 18, cells, LANES), f32),
            vmem((cells, LANES), f32),
            vmem((cells, LANES), jnp.int32),
            pltpu.SMEM((2, 8), f32),
            pltpu.SMEM((3, 8), f32),
            pltpu.SMEM((3, 8), f32),
            vmem((1, nsrc), jnp.int32),
            vmem((3, 2, nsrc), f32),
            vmem((1, nrec), jnp.int32),
            vmem((3, 2, nrec), f32),
            vmem((2, 2, 6, NRAD, NAZ + 16, LANES), f32),
            vmem((2, 2, 3, NRAD, NAZ + 16, LANES), f32),
            vmem((2, 6) + block, f32),
            vmem((2, 3) + block, f32),
            vmem((2, 4, 2, 5, NAZ, LANES), f32),
            vmem((2, 4, 2, 5, NAZ, LANES), f32),
            vmem((2, 2, 2, 4, 8, LANES), f32),
            vmem((2, 2, 2, 4, 8, LANES), f32),
            vmem((2, 2, NAZ, LANES), f32),
            vmem((2, 2, 2, NAZ, LANES), f32),
            vmem((2, 4, 2, 3, 8, LANES), f32),
            vmem((2, 4, 2, 3, 8, LANES), f32),
            vmem((2, 4, 8, LANES), f32),
            vmem((2, 4, 8, LANES), f32),
            vmem((2, 1, 6) + block, f32),
            vmem((2, 6) + block, f32),
            vmem((6,) + block, f32),
            vmem((2, 2, 3) + block, f32),
            vmem((4,) + block, f32),
            vmem((8,) + block, f32),
            pltpu.SemaphoreType.DMA((16,)),
            pltpu.SemaphoreType.DMA((2, 4, 7)),
            pltpu.SemaphoreType.DMA((2, 4, 7)),
            pltpu.SemaphoreType.DMA((2, 2)),
        ],
        compiler_params=pltpu.CompilerParams(
            collective_id=0, has_side_effects=True, vmem_limit_bytes=60 * 2**20
        ),
        name="window",
    )(
        forward_state.reshape(9, cells, LANES),
        forward_memory.reshape(18, cells, LANES),
        adjoint_state.reshape(9, cells, LANES),
        adjoint_memory.reshape(18, cells, LANES),
        shear_modulus.reshape(cells, LANES),
        zone.reshape(cells, LANES),
        zone_elastic, zone_rates, zone_weights,
        source_cells.reshape(1, nsrc), source_force.transpose(1, 0, 2),
        receiver_cells.reshape(1, nrec), receiver_residual.transpose(1, 0, 2),
    )
    gradient, adjoint_out = pl.pallas_call(
        hand_on,
        out_shape=(
            jax.ShapeDtypeStruct((cells, LANES), f32),
            jax.ShapeDtypeStruct((9, cells, LANES), f32),
        ),
        in_specs=[pl.BlockSpec(memory_space=pl.ANY)] * 2,
        out_specs=(hbm, hbm),
        scratch_shapes=[pltpu.SemaphoreType.DMA((2,))],
        compiler_params=pltpu.CompilerParams(vmem_limit_bytes=2**20),
        name="hand_on",
    )(gradient, adjoint_out)
    return gradient.reshape(NAZ, NRAD, LANES), adjoint_out.reshape(9, NAZ, NRAD, LANES)


def solution(mesh):
    return jax.shard_map(
        shards,
        mesh=mesh,
        in_specs=(
            P(None, "az", "rad", "dep"),
            P(None, None, "az", "rad", "dep"),
            P(None, "az", "rad", "dep"),
            P(None, None, "az", "rad", "dep"),
            P("az", "rad", "dep"),
            P("az", "rad", "dep"),
            P(), P(), P(), P(), P(), P(), P(),
        ),
        out_specs=(P("az", "rad", "dep"), P(None, "az", "rad", "dep")),
        check_vma=False,
    )
```

```python
import math

import jax
import jax.numpy as jnp
from jax import lax
from jax.experimental import pallas as pl
from jax.experimental.pallas import tpu as pltpu
from jax.sharding import PartitionSpec as P

MESH = pl.DeviceIdType.MESH
f32 = jnp.float32

DT = 0.2
C1 = 1.125
C2 = 1.0 / 24.0

RR, RZ, RT, TT, TZ, ZZ = range(6)
IN_STATE = {RR: 3, TT: 4, ZZ: 5, RT: 6, RZ: 7, TZ: 8}
STRAIN_ORDER = (RR, TT, ZZ, RT, RZ, TZ)

ADJ, FWD = 0, 1
NAZ, NRAD, LANES = 16, 4, 128
LO, HI = 8, 8 + NAZ
STRESS_PLAN = (((RR, 3), (RZ, 2), (RZ, 3), (RT, 2), (RT, 3)), ((RR, 0), (RR, 1), (RZ, 0), (RT, 0)))
VEL_PLAN = (((0, 2), (0, 3), (1, 3), (2, 3)), ((0, 0), (1, 0), (1, 1), (2, 0), (2, 1)))


STRESS_AHEAD, VEL_AHEAD = (False, False, True), (False, True, True)
STRESS_AZ_AHEAD, VEL_AZ_AHEAD = (False, True, False), (True, False, True)


class View:
    def __init__(self, ref, sys, step):
        self.ref, self.lead = ref, (sys, step)

    def __getitem__(self, index):
        return self.ref[self.lead + index]

    def __setitem__(self, index, value):
        self.ref[self.lead + index] = value


def forward4(before, here, after, after2):
    return C1 * (after - here) - C2 * (after2 - before)


def backward4(before2, before, here, after):
    return C1 * (here - before) - C2 * (after - before2)


def kernel(
    fs, fm, as_, am, mu_h, zone_h, ze_h, zr_h, zw_h, sc_h, sf_h, rc_h, rr_h,
    grad_v, out_v,
    raw, mem, mu_v, zone_v, ze, zr, zw, sc_v, sf_v, rc_v, rr_v,
    stress, vel, acc, azc, rad_out, rad_in, az_out, az_in, msg_out, msg_in, strain, a1, a2, inj, geo, mat,
    in_sem, send_sem, recv_sem,
):
    n_az, n_rad, n_dep = lax.axis_size("az"), lax.axis_size("rad"), lax.axis_size("dep")
    az, rad, dep = lax.axis_index("az"), lax.axis_index("rad"), lax.axis_index("dep")
    az_up, az_dn = {"az": lax.rem(az + 1, n_az)}, {"az": lax.rem(az + n_az - 1, n_az)}
    rad_up, rad_dn = {"rad": rad + 1}, {"rad": rad - 1}
    dep_other = {"dep": 1 - dep}

    has_dn, has_up = rad > 0, rad < n_rad - 1
    barrier = pltpu.get_barrier_semaphore()
    for place in (az_up, az_dn, dep_other):
        pl.semaphore_signal(barrier, inc=1, device_id=place, device_id_type=MESH)

    @pl.when(has_up)
    def _():
        pl.semaphore_signal(barrier, inc=1, device_id=rad_up, device_id_type=MESH)

    @pl.when(has_dn)
    def _():
        pl.semaphore_signal(barrier, inc=1, device_id=rad_dn, device_id_type=MESH)

    pending = []

    def bring(src, dst):
        copy = pltpu.make_async_copy(src, dst, in_sem.at[len(pending)])
        copy.start()
        pending.append(copy)
        return copy

    states = (as_, fs)
    memories = (am, fm)
    got_stress = [bring(states[s].at[pl.ds(3, 6)], raw.at[s, pl.ds(3, 6)]) for s in (ADJ, FWD)]

    lane = lax.broadcasted_iota(jnp.int32, (NAZ, LANES), 1)
    lane8 = lax.broadcasted_iota(jnp.int32, (8, LANES), 1)

    def where_f(cond, value):
        return jnp.where(cond, f32(value), f32(0.0))

    def base(t, r, half):
        return 12 * (2 * r + half) + 4 * t

    ends = (lane8 < 2) | (lane8 >= 126)

    def pack_depth(sys, phase, gets):
        parcel = None
        for r in range(NRAD):
            for t, get in enumerate(gets):
                g = get(r)
                for half in range(2):
                    piece = jnp.where(ends, g[8 * half: 8 * half + 8], 0.0)
                    if base(t, r, half):
                        piece = pltpu.roll(piece, base(t, r, half), 1)
                    parcel = piece if parcel is None else parcel + piece
        msg_out[sys, phase] = parcel

    def depth_local(g, ahead):
        m1 = pltpu.roll(g, LANES - 1, 1)
        r1 = pltpu.roll(g, 1, 1)
        if ahead:
            m2 = pltpu.roll(g, LANES - 2, 1)
            return (where_f(lane < 127, C1) * m1 - C1 * g - where_f(lane < 126, C2) * m2
                    + where_f(lane >= 1, C2) * r1)
        r2 = pltpu.roll(g, 2, 1)
        return (C1 * g - where_f(lane >= 1, C1) * r1 - where_f(lane < 127, C2) * m1
                + where_f(lane >= 2, C2) * r2)

    slot = lax.rem(lax.rem(lane8 + 2, LANES), 12)
    place_in = lax.rem(slot, 4)
    which = lax.div(slot, 4)

    def wraps(sys, phase, aheads):
        x = msg_in[sys, phase]
        ahead = None
        for t in range(3):
            if aheads[t]:
                ahead = (which == t) if ahead is None else ahead | (which == t)
        behind = jnp.logical_not(ahead)
        m1, m2 = pltpu.roll(x, LANES - 1, 1), pltpu.roll(x, LANES - 2, 1)
        r1, r2 = pltpu.roll(x, 1, 1), pltpu.roll(x, 2, 1)
        at126, at127, at0, at1 = [place_in == i for i in range(4)]
        k_m1 = jnp.where(at127, jnp.where(ahead, f32(C1), f32(-C2)), 0.0)
        k_m2 = where_f(ahead & (at126 | at127), -C2)
        k_r1 = jnp.where(at0, jnp.where(ahead, f32(C2), f32(-C1)), 0.0)
        k_r2 = where_f(behind & (at0 | at1), C2)
        return k_m1 * m1 + k_m2 * m2 + k_r1 * r1 + k_r2 * r2

    mine = lane8 - 126 * (1 - dep)
    edge = (mine >= 0) & (mine < 2)

    def depth_halo(parcel, t, r):
        halves = []
        for half in range(2):
            shift = base(t, r, half)
            piece = pltpu.roll(parcel, LANES - shift, 1) if shift else parcel
            halves.append(jnp.where(edge, piece, 0.0))
        return jnp.concatenate(halves, axis=0)

    started = []

    def plan_of(phase):
        return VEL_PLAN if phase % 2 else STRESS_PLAN

    def keep(sys, phase, c, r, value):
        ref = vel if phase % 2 else stress
        ref[sys, phase // 2, c, r, LO:HI] = value
        for way in range(2):
            if (c, r) in plan_of(phase)[way]:
                rad_out[sys, phase, way, plan_of(phase)[way].index((c, r))] = value

    def exchange(sys, phase, field, az_from, gets):
        number = [0]
        legs, up_legs, dn_legs = [], [], []

        def leg(src, dst, place, group):
            n = number[0]
            number[0] += 1

            def make():
                return pltpu.make_async_remote_copy(
                    src_ref=src(), dst_ref=dst(),
                    send_sem=send_sem.at[sys, phase, n], recv_sem=recv_sem.at[sys, phase, n],
                    device_id=place, device_id_type=MESH,
                )

            make().start()
            group.append(make)

        def layers(ref, way):
            return lambda: ref.at[sys, phase, way, pl.ds(0, len(plan_of(phase)[way]))]

        @pl.when(has_up)
        def _():
            leg(layers(rad_out, 0), layers(rad_in, 0), rad_up, up_legs)

        @pl.when(has_dn)
        def _():
            leg(layers(rad_out, 1), layers(rad_in, 1), rad_dn, dn_legs)

        for way, row, place in ((0, HI - 2, az_up), (1, LO, az_dn)):
            for i in range(3):
                for r in range(NRAD):
                    az_out[sys, phase, way, i, 2 * r: 2 * r + 2] = field[az_from + i, r, row: row + 2]
            leg(lambda way=way: az_out.at[sys, phase, way], lambda way=way: az_in.at[sys, phase, way],
                place, legs)
        pack_depth(sys, phase, gets)
        leg(lambda: msg_out.at[sys, phase], lambda: msg_in.at[sys, phase], dep_other, legs)
        groups = legs, up_legs, dn_legs, (sys, phase)
        started.append(groups)
        return groups

    even = lax.rem(lax.broadcasted_iota(jnp.int32, (8, LANES), 0), 2) == 0

    def arrive(groups):
        legs, up_legs, dn_legs, (sys, phase) = groups
        for make in legs:
            make().wait_recv()
        for i, ahead in enumerate(VEL_AZ_AHEAD if phase % 2 else STRESS_AZ_AHEAD):
            low, high = az_in[sys, phase, 0, i], az_in[sys, phase, 1, i]
            if ahead:
                low = jnp.where(even, C2 * pltpu.roll(low, 7, 0), 0.0)
                high = jnp.where(even, 0.0, C1 * pltpu.roll(high, 1, 0)) - C2 * high
            else:
                low = C2 * low - jnp.where(even, C1 * pltpu.roll(low, 7, 0), 0.0)
                high = jnp.where(even, 0.0, -C2 * pltpu.roll(high, 1, 0))
            az_in[sys, phase, 0, i] = low
            az_in[sys, phase, 1, i] = high
            for r in range(NRAD):
                azc[sys, i, r, 0:2] = az_in[sys, phase, 0, i, 2 * r: 2 * r + 2]
                azc[sys, i, r, NAZ - 2: NAZ] = az_in[sys, phase, 1, i, 2 * r: 2 * r + 2]

        @pl.when(has_dn)
        def _():
            for make in up_legs:
                make().wait_recv()

        @pl.when(has_up)
        def _():
            for make in dn_legs:
                make().wait_recv()

    def rows(r):
        return pl.ds(r, NAZ, stride=NRAD)

    def stress_field(sys, step):
        return View(stress, sys, step)

    def vel_field(sys, step):
        return View(vel, sys, step)

    def stress_gets(sys, step):
        field = stress_field(sys, step)
        return [lambda r, c=c: field[c, r, LO:HI] for c in (RZ, TZ, ZZ)]

    def vel_gets(sys, step):
        field = vel_field(sys, step)
        return [lambda r, c=c: field[c, r, LO:HI] for c in (2, 0, 1)]

    def send_stress(sys, step):
        return exchange(sys, 2 * step, stress_field(sys, step), RT, stress_gets(sys, step))

    def send_vel(sys, step):
        return exchange(sys, 2 * step + 1, vel_field(sys, step), 0, vel_gets(sys, step))

    def rad_local(sys, phase, c, r, ahead):
        field = vel if phase % 2 else stress

        def own(k):
            return field[sys, phase // 2, c, k, LO:HI]

        first = -1 if ahead else -2
        factors = {first: C2, first + 1: -C1, first + 2: C1, first + 3: -C2}
        total = None
        for shift, factor in factors.items():
            if 0 <= r + shift < NRAD:
                term = factor * own(r + shift)
                total = term if total is None else total + term
        return total

    def rad_halo(sys, phase, c, r, ahead):
        up, down = plan_of(phase)
        first = -1 if ahead else -2
        factors = {first: C2, first + 1: -C1, first + 2: C1, first + 3: -C2}
        total = None
        for shift, factor in factors.items():
            k = r + shift
            if 0 <= k < NRAD:
                continue
            way, row = (0, up.index((c, k + NRAD))) if k < 0 else (1, down.index((c, k - NRAD)))
            term = factor * rad_in[sys, phase, way, row]
            total = term if total is None else total + term
        return total

    def plus(*terms):
        terms = [t for t in terms if t is not None]
        total = terms[0]
        for t in terms[1:]:
            total = total + t
        return total

    def az4(field, c, r, first):
        return [field[c, r, LO + first + i: HI + first + i] for i in range(4)]

    def velocity_local(sys, step):
        field, phase = stress_field(sys, step), 2 * step
        gets = stress_gets(sys, step)
        for r in range(NRAD):
            inv_s, inv_c, inv_sa, inv_ca = [geo[i, r] for i in range(4)]
            if step == 0:
                old = [raw[sys, c, rows(r)] for c in range(3)]
            else:
                old = [vel[sys, 0, c, r, LO:HI] for c in range(3)]
            s_rr, s_tt = field[RR, r, LO:HI], field[TT, r, LO:HI]
            s_rt, s_rz = field[RT, r, LO:HI], field[RZ, r, LO:HI]
            push = [
                rad_local(sys, phase, RR, r, True) + backward4(*az4(field, RT, r, -2)) * inv_sa
                + depth_local(gets[0](r), False) + (s_rr - s_tt) * inv_s,
                rad_local(sys, phase, RT, r, False) + forward4(*az4(field, TT, r, -1)) * inv_ca
                + depth_local(gets[1](r), False) + 2.0 * s_rt * inv_c,
                rad_local(sys, phase, RZ, r, False) + backward4(*az4(field, TZ, r, -2)) * inv_ca
                + depth_local(gets[2](r), True) + s_rz * inv_c,
            ]
            gain = mat[0, r]
            for c in range(3):
                acc[sys, c, r] = old[c] + gain * (push[c] + inj[sys, step, c, r])

    def velocity_finish(sys, step):
        phase = 2 * step
        parcel = wraps(sys, phase, STRESS_AHEAD)
        for r in range(NRAD):
            gain = mat[0, r]
            inv = (geo[2, r], geo[3, r], geo[3, r])
            for c, (s, ahead) in enumerate(((RR, True), (RT, False), (RZ, False))):
                halo = plus(azc[sys, c, r] * inv[c], depth_halo(parcel, c, r),
                            rad_halo(sys, phase, s, r, ahead))
                keep(sys, phase + 1, c, r, acc[sys, c, r] + gain * halo)

    def strain_local(sys, step):
        field, phase = vel_field(sys, step), 2 * step + 1
        gets = vel_gets(sys, step)
        for r in range(NRAD):
            inv_s, inv_c, inv_sa, inv_ca = [geo[i, r] for i in range(4)]
            v_r, v_t = field[0, r, LO:HI], field[1, r, LO:HI]
            acc[sys, 0, r] = rad_local(sys, phase, 0, r, False)
            acc[sys, 1, r] = backward4(*az4(field, 1, r, -2)) * inv_ca + v_r * inv_c
            acc[sys, 2, r] = depth_local(gets[0](r), False)
            acc[sys, 3, r] = 0.5 * (rad_local(sys, phase, 1, r, True)
                                    + forward4(*az4(field, 0, r, -1)) * inv_sa - v_t * inv_s)
            acc[sys, 4, r] = 0.5 * (depth_local(gets[1](r), True) + rad_local(sys, phase, 2, r, True))
            acc[sys, 5, r] = 0.5 * (depth_local(gets[2](r), True)
                                    + forward4(*az4(field, 2, r, -1)) * inv_ca)

    def strain_at(sys, step, parcel, r):
        phase = 2 * step + 1
        inv_sa, inv_ca = geo[2, r], geo[3, r]
        halo = [
            rad_halo(sys, phase, 0, r, False),
            azc[sys, 1, r] * inv_ca,
            depth_halo(parcel, 0, r),
            0.5 * plus(azc[sys, 0, r] * inv_sa, rad_halo(sys, phase, 1, r, True)),
            0.5 * plus(depth_halo(parcel, 1, r), rad_halo(sys, phase, 2, r, True)),
            0.5 * (depth_halo(parcel, 2, r) + azc[sys, 2, r] * inv_ca),
        ]
        return [plus(acc[sys, i, r], halo[i]) for i in range(6)]

    def load_state(sys):
        got_stress[sys].wait()
        for c in range(6):
            for r in range(NRAD):
                keep(sys, 0, c, r, raw[sys, IN_STATE[c], rows(r)])

    load_state(ADJ)
    pl.semaphore_wait(barrier, 3 + has_up.astype(jnp.int32) + has_dn.astype(jnp.int32))
    legs_s = [None, None]
    legs_v = [None, None]
    legs_s[ADJ] = send_stress(ADJ, 0)
    load_state(FWD)
    legs_s[FWD] = send_stress(FWD, 0)
    got_small = [
        bring(a, b)
        for a, b in (
            (ze_h, ze), (zr_h, zr), (zw_h, zw), (sc_h, sc_v), (sf_h, sf_v), (rc_h, rc_v),
            (rr_h, rr_v), (zone_h, zone_v), (mu_h, mu_v),
        )
    ]
    got_vel = [bring(states[s].at[pl.ds(0, 3)], raw.at[s, pl.ds(0, 3)]) for s in (ADJ, FWD)]
    got_mem = [bring(memories[s], mem.at[s]) for s in (ADJ, FWD)]

    @pl.when(rad == 0)
    def _():
        rad_in[:, :, 0] = jnp.zeros((2, 4, 5, NAZ, LANES), f32)

    @pl.when(rad == n_rad - 1)
    def _():
        rad_in[:, :, 1] = jnp.zeros((2, 4, 5, NAZ, LANES), f32)

    for copy in got_small:
        copy.wait()
    angle = 2.0 * math.pi / (NAZ * n_az)
    inner = (NAZ * n_az) / (2.0 * math.pi)
    for r in range(NRAD):
        centre = jnp.full((NAZ, LANES), f32(inner), f32) + (rad * NRAD + r).astype(f32)
        staggered = centre + 0.5
        geo[0, r] = 1.0 / staggered
        geo[1, r] = 1.0 / centre
        geo[2, r] = 1.0 / (staggered * angle)
        geo[3, r] = 1.0 / (centre * angle)

    betas = []
    for r in range(NRAD):
        zone = zone_v[rows(r)]
        looked = [jnp.zeros((NAZ, LANES), f32) for _ in range(8)]
        for number in range(8):
            hit = zone == number
            for t in range(8):
                ref, row = (ze, t) if t < 2 else (zr, t - 2) if t < 5 else (zw, t - 5)
                looked[t] = jnp.where(hit, ref[row, number], looked[t])
        lame, buoyancy = looked[0], looked[1]
        alpha = [DT * looked[2 + i] for i in range(3)]
        weight = looked[5:8]
        beta = [1.0 - a for a in alpha]
        share = [a * w for a, w in zip(alpha, weight)]
        gain = DT * (1.0 - (share[0] + share[1] + share[2]))
        later = DT * (beta[0] * share[0] + beta[1] * share[1] + beta[2] * share[2])
        doubled = 2.0 * mu_v[rows(r)]
        mat[0, r] = DT * buoyancy
        mat[1, r] = gain * lame
        mat[2, r] = gain * doubled
        mat[3, r] = later * lame
        mat[4, r] = later * doubled
        for i in range(3):
            mat[5 + i, r] = beta[i]

    def inject(sys, cells_ref, force_ref, count):
        cells = cells_ref[...]
        around = lax.shift_right_logical(cells, 13) - NAZ * az
        radial = (lax.shift_right_logical(cells, 8) & 31) - NRAD * rad
        depth = (cells & 255) - LANES * dep
        inside = (around >= 0) & (around < NAZ) & (radial >= 0) & (radial < NRAD)
        key = jnp.where(inside, radial * NAZ + around, -1)
        here = lax.broadcasted_iota(jnp.int32, (NRAD * NAZ, count), 0) == key
        lanes = (lax.broadcasted_iota(jnp.int32, (LANES, count), 0) == depth).astype(f32)
        for step in range(2):
            for c in range(3):
                picked = jnp.where(here, force_ref[c, step: step + 1, :], 0.0)
                total = lax.dot_general(
                    picked, lanes, (((1,), (1,)), ((), ())),
                    precision=lax.Precision.HIGHEST, preferred_element_type=f32,
                )
                for r in range(NRAD):
                    inj[sys, step, c, r] = total[r * NAZ: (r + 1) * NAZ]

    inject(ADJ, rc_v, rr_v, rc_v.shape[1])
    inject(FWD, sc_v, sf_v, sc_v.shape[1])
    for sys in (ADJ, FWD):
        got_vel[sys].wait()
        azc[sys] = jnp.zeros((3, NRAD, NAZ, LANES), f32)
        for step in range(2):
            for row in (0, HI):
                stress[sys, step, RT: RT + 3, :, row: row + 8] = jnp.zeros((3, NRAD, 8, LANES), f32)
                vel[sys, step, :, :, row: row + 8] = jnp.zeros((3, NRAD, 8, LANES), f32)
        velocity_local(sys, 0)

    def advance_velocity(sys, step):
        arrive(legs_s[sys])
        velocity_finish(sys, step)
        legs_v[sys] = send_vel(sys, step)

    for sys in (ADJ, FWD):
        advance_velocity(sys, 0)
    for sys in (ADJ, FWD):
        strain_local(sys, 0)

    for sys in (ADJ, FWD):
        got_mem[sys].wait()
        for r in range(NRAD):
            beta = [mat[5 + i, r] for i in range(3)]
            for e in range(6):
                m = [beta[i] * mem[sys, 6 * i + e, rows(r)] for i in range(3)]
                a1[sys, e, r] = raw[sys, 3 + e, rows(r)] - DT * (m[0] + m[1] + m[2])
                if sys == ADJ:
                    a2[e, r] = DT * (beta[0] * m[0] + beta[1] * m[1] + beta[2] * m[2])

    def first_stress(sys):
        arrive(legs_v[sys])
        parcel = wraps(sys, 1, VEL_AHEAD)
        for r in range(NRAD):
            e = strain_at(sys, 0, parcel, r)
            dilation = e[0] + e[1] + e[2]
            common = mat[1, r] * dilation
            gm = mat[2, r]
            for i in range(6):
                strain[sys, 0, i, r] = e[i]
                change = gm * e[i] + common if i < 3 else gm * e[i]
                keep(sys, 2, STRAIN_ORDER[i], r, a1[sys, i, r] + change)
        legs_s[sys] = send_stress(sys, 1)

    for sys in (ADJ, FWD):
        first_stress(sys)
    for sys in (ADJ, FWD):
        velocity_local(sys, 1)

    for r in range(NRAD):
        e = [strain[ADJ, 0, i, r] for i in range(6)]
        common = mat[3, r] * (e[0] + e[1] + e[2])
        hm = mat[4, r]
        for i in range(6):
            drop = hm * e[i] + common if i < 3 else hm * e[i]
            a2[i, r] = stress[ADJ, 1, STRAIN_ORDER[i], r, LO:HI] - a2[i, r] - drop

    for sys in (ADJ, FWD):
        advance_velocity(sys, 1)
    for sys in (ADJ, FWD):
        strain_local(sys, 1)
    for r in range(NRAD):
        for c in range(3):
            out_v[c, rows(r)] = vel[ADJ, 1, c, r, LO:HI]

    def product(e, f):
        return 2.0 * DT * (e[0] * f[0] + e[1] * f[1] + e[2] * f[2]
                           + 2.0 * (e[3] * f[3] + e[4] * f[4] + e[5] * f[5]))

    def sent(batch):
        for legs, _, _, _ in batch:
            for make in legs:
                make().wait_send()

        @pl.when(has_up)
        def _():
            for _, up_legs, _, _ in batch:
                for make in up_legs:
                    make().wait_send()

        @pl.when(has_dn)
        def _():
            for _, _, dn_legs, _ in batch:
                for make in dn_legs:
                    make().wait_send()

    sent(started[:6])
    arrive(legs_v[ADJ])
    parcel = wraps(ADJ, 3, VEL_AHEAD)
    for r in range(NRAD):
        e = strain_at(ADJ, 1, parcel, r)
        common = mat[1, r] * (e[0] + e[1] + e[2])
        gm = mat[2, r]
        for i in range(6):
            change = gm * e[i] + common if i < 3 else gm * e[i]
            out_v[3 + i, rows(r)] = a2[i, r] + change
        a1[ADJ, 0, r] = product(e, [strain[FWD, 0, i, r] for i in range(6)])

    arrive(legs_v[FWD])
    parcel = wraps(FWD, 3, VEL_AHEAD)
    for r in range(NRAD):
        e = strain_at(FWD, 1, parcel, r)
        grad_v[rows(r)] = a1[ADJ, 0, r] + product(e, [strain[ADJ, 0, i, r] for i in range(6)])

    sent(started[6:])


def hand_on(grad_in, adj_in, grad_out, adj_out, sems):
    copies = [pltpu.make_async_copy(adj_in, adj_out, sems.at[0]),
              pltpu.make_async_copy(grad_in, grad_out, sems.at[1])]
    for copy in copies:
        copy.start()
    for copy in copies:
        copy.wait()


def shards(
    forward_state, forward_memory, adjoint_state, adjoint_memory, shear_modulus, zone,
    zone_elastic, zone_rates, zone_weights, source_cells, source_force, receiver_cells,
    receiver_residual,
):
    cells = NAZ * NRAD
    nsrc, nrec = source_cells.shape[0], receiver_cells.shape[0]
    block = (NRAD, NAZ, LANES)
    vmem = pltpu.VMEM
    hbm = pl.BlockSpec(memory_space=pltpu.HBM)
    gradient, adjoint_out = pl.pallas_call(
        kernel,
        out_shape=(vmem((cells, LANES), f32), vmem((9, cells, LANES), f32)),
        in_specs=[hbm] * 13,
        out_specs=(pl.BlockSpec(memory_space=pltpu.VMEM),) * 2,
        scratch_shapes=[
            vmem((2, 9, cells, LANES), f32),
            vmem((2, 18, cells, LANES), f32),
            vmem((cells, LANES), f32),
            vmem((cells, LANES), jnp.int32),
            pltpu.SMEM((2, 8), f32),
            pltpu.SMEM((3, 8), f32),
            pltpu.SMEM((3, 8), f32),
            vmem((1, nsrc), jnp.int32),
            vmem((3, 2, nsrc), f32),
            vmem((1, nrec), jnp.int32),
            vmem((3, 2, nrec), f32),
            vmem((2, 2, 6, NRAD, NAZ + 16, LANES), f32),
            vmem((2, 2, 3, NRAD, NAZ + 16, LANES), f32),
            vmem((2, 6) + block, f32),
            vmem((2, 3) + block, f32),
            vmem((2, 4, 2, 5, NAZ, LANES), f32),
            vmem((2, 4, 2, 5, NAZ, LANES), f32),
            vmem((2, 4, 2, 3, 8, LANES), f32),
            vmem((2, 4, 2, 3, 8, LANES), f32),
            vmem((2, 4, 8, LANES), f32),
            vmem((2, 4, 8, LANES), f32),
            vmem((2, 1, 6) + block, f32),
            vmem((2, 6) + block, f32),
            vmem((6,) + block, f32),
            vmem((2, 2, 3) + block, f32),
            vmem((4,) + block, f32),
            vmem((8,) + block, f32),
            pltpu.SemaphoreType.DMA((16,)),
            pltpu.SemaphoreType.DMA((2, 4, 5)),
            pltpu.SemaphoreType.DMA((2, 4, 5)),
        ],
        compiler_params=pltpu.CompilerParams(
            collective_id=0, has_side_effects=True, vmem_limit_bytes=60 * 2**20
        ),
        name="window",
    )(
        forward_state.reshape(9, cells, LANES),
        forward_memory.reshape(18, cells, LANES),
        adjoint_state.reshape(9, cells, LANES),
        adjoint_memory.reshape(18, cells, LANES),
        shear_modulus.reshape(cells, LANES),
        zone.reshape(cells, LANES),
        zone_elastic, zone_rates, zone_weights,
        source_cells.reshape(1, nsrc), source_force.transpose(1, 0, 2),
        receiver_cells.reshape(1, nrec), receiver_residual.transpose(1, 0, 2),
    )
    gradient, adjoint_out = pl.pallas_call(
        hand_on,
        out_shape=(
            jax.ShapeDtypeStruct((cells, LANES), f32),
            jax.ShapeDtypeStruct((9, cells, LANES), f32),
        ),
        in_specs=[pl.BlockSpec(memory_space=pl.ANY)] * 2,
        out_specs=(hbm, hbm),
        scratch_shapes=[pltpu.SemaphoreType.DMA((2,))],
        compiler_params=pltpu.CompilerParams(vmem_limit_bytes=2**20),
        name="hand_on",
    )(gradient, adjoint_out)
    return gradient.reshape(NAZ, NRAD, LANES), adjoint_out.reshape(9, NAZ, NRAD, LANES)


def solution(mesh):
    return jax.shard_map(
        shards,
        mesh=mesh,
        in_specs=(
            P(None, "az", "rad", "dep"),
            P(None, None, "az", "rad", "dep"),
            P(None, "az", "rad", "dep"),
            P(None, None, "az", "rad", "dep"),
            P("az", "rad", "dep"),
            P("az", "rad", "dep"),
            P(), P(), P(), P(), P(), P(), P(),
        ),
        out_specs=(P("az", "rad", "dep"), P(None, "az", "rad", "dep")),
        check_vma=False,
    )
```
